32 devices in a mesh: blade: 4 (over y, x), span: 8 (over z, core).
Axes of the slice: x: 2, y: 2, z: 4, core: 2. Of those that a mesh axis runs over, the one named last changes fastest.
Arguments:
- adj_source: float32 [8, 1024, 1024], P(None, 'blade', 'span'), may hold values from -4 to 4
- face_flux: float32 [8, 32768], P(None, ('blade', 'span')), may hold values from -6 to 6
- face_owner: int32 [32768], P(('blade', 'span')), may hold values from 0 to 3, as said below
- face_cell: int32 [32768], P(('blade', 'span')), may hold values from 0 to 32767
- block_inverse: float32 [1024, 128], P('span'), may hold values from -4 to 4
- carry_gain: float32 [1024, 128], P('span'), may hold values from -1 to 1
Outputs:
- adjoint: float32 [8, 1024, 1024], P(None, 'blade', 'span')
The draws below stay inside these ranges and needn't reach their ends.
Inputs may be any that keep to these rules, and one draw needn't show every extreme that they name: `face_owner`: the faces of one device name each owner at most 512 times; in every group of devices of one span index, one owner is named exactly 512 times by each of its devices.
All inputs are finite; a program needn't handle non-finite values.
Results may differ from the reference program's by a relative error of at most 0.0001.
Values sent between devices are 32-bit elements; how exact they have to be, the bound alone decides.
No kernel may reach another device: no remote copies, remote signals or barrier semaphores. Data moves between devices by JAX's collectives and lax.ppermute only.
A program may use at most 128 MiB of HBM per device.

```python
import jax
import jax.numpy as jnp
from jax import lax

HR = 8
CIRC = 256
RAD_DEV = 128
F_DEV = 1024
CAP = 512
ITERS = 3
NC = 1024
NRAD = 1024
CELLS = 32768
FACES = 32768
N_BLADE = 4
N_SPAN = 8


def shuffle_row(subkey, owner_row):
    return jax.random.permutation(subkey, owner_row)


def draw_face_owner(key, part):
    key = jax.random.fold_in(key, 11)
    nblocks = FACES // F_DEV
    heavy_span = jax.random.randint(jax.random.fold_in(key, 1), (N_SPAN,), 0, N_BLADE)
    heavy = heavy_span[jnp.arange(nblocks) % N_SPAN]
    others = jax.random.randint(jax.random.fold_in(key, 2), (nblocks, F_DEV - CAP), 0, N_BLADE - 1)
    owners = jnp.concatenate([jnp.broadcast_to(heavy[:, None], (nblocks, CAP)), (heavy[:, None] + 1 + others) % N_BLADE], axis=1).astype(jnp.int32)
    subkeys = jax.random.split(jax.random.fold_in(key, 3), nblocks)
    mixed = jax.vmap(shuffle_row)(subkeys, owners)
    return mixed.reshape(FACES).astype(jnp.int32)


def draw_block_inverse(key, part):
    key = jax.random.fold_in(key, 23)
    nblocks = NRAD // RAD_DEV
    shape = (nblocks, RAD_DEV, RAD_DEV)
    spread = jax.random.normal(jax.random.fold_in(key, 1), shape, jnp.float32) * (0.5 * RAD_DEV ** (-0.5))
    diagonal = jax.random.uniform(jax.random.fold_in(key, 2), (nblocks, RAD_DEV), jnp.float32, 0.7, 1.4)
    row_ids = jnp.arange(RAD_DEV)[:, None]
    col_ids = jnp.arange(RAD_DEV)[None, :]
    matrix = jnp.where((row_ids == col_ids)[None, :, :], diagonal[:, :, None], jnp.clip(spread, -4.0, 4.0))
    return matrix.reshape(NRAD, RAD_DEV).astype(jnp.float32)


def draw_carry_gain(key, part):
    key = jax.random.fold_in(key, 37)
    nblocks = NRAD // RAD_DEV
    shape = (nblocks, RAD_DEV, RAD_DEV)
    spread = jax.random.normal(jax.random.fold_in(key, 1), shape, jnp.float32) * (0.22 * RAD_DEV ** (-0.5))
    diagonal = jnp.exp(jax.random.uniform(jax.random.fold_in(key, 2), (nblocks, RAD_DEV), jnp.float32, -1.6, -0.05))
    row_ids = jnp.arange(RAD_DEV)[:, None]
    col_ids = jnp.arange(RAD_DEV)[None, :]
    matrix = jnp.where((row_ids == col_ids)[None, :, :], diagonal[:, :, None], jnp.clip(spread, -0.9, 0.9))
    return matrix.reshape(NRAD, RAD_DEV).astype(jnp.float32)


def place_ends(entries, rng, low, largest):
    longest = entries.shape.index(max(entries.shape))
    spots = []
    for shift in (0, 1):
        where = [jax.random.randint(jax.random.fold_in(rng, axis), (), 0, length) for axis, length in enumerate(entries.shape)]
        where[longest] = (where[longest] + shift) % entries.shape[longest]
        spots.append(tuple(where))
    return entries.at[spots[0]].set(low).at[spots[1]].set(largest)


def steps_of(rng, shape, shards, smallest, largest):
    level, own = 1.0, jax.random.fold_in(rng, 6)
    for axis_at, blocks in shards:
        steps = jnp.exp(jax.random.uniform(jax.random.fold_in(own, axis_at), (blocks,), jnp.float32, smallest / len(shards), largest / len(shards)))
        level = level * jnp.repeat(steps, shape[axis_at] // blocks).reshape([-1 if axis == axis_at else 1 for axis in range(len(shape))])
    return level


def scatter_about(key, extent, width, reach, shards=(), held_as=jnp.bfloat16):
    values = jax.random.normal(key, extent, jnp.float32) * width
    if len(shards) > 0:
        values = steps_of(key, extent, shards, -0.22, 0.18) * values
    return jnp.clip(values, min=-reach, max=reach).astype(held_as)


def setup_inputs(seed: int = 0) -> dict:
    streams_of = jax.random.split(jax.random.key(seed), 7)
    adj_source = scatter_about(streams_of[0], (HR, NC, NRAD), 0.5, 4.0, ((1, 4), (2, 8)), jnp.float32)
    face_flux = scatter_about(streams_of[1], (HR, FACES), 1.0, 6.0, ((1, 32),), jnp.float32)
    face_owner = draw_face_owner(jax.random.fold_in(streams_of[6], 71), 0)
    face_cell = place_ends(jax.random.randint(streams_of[3], (FACES,), 0, CELLS), jax.random.fold_in(streams_of[3], 1), 0, CELLS - 1).astype(jnp.int32)
    block_inverse = draw_block_inverse(jax.random.fold_in(streams_of[6], 71), 0)
    carry_gain = draw_carry_gain(jax.random.fold_in(streams_of[6], 71), 0)
    return {"adj_source": adj_source, "face_flux": face_flux, "face_owner": face_owner, "face_cell": face_cell, "block_inverse": block_inverse, "carry_gain": carry_gain}


coupling = 0.05
highest = lax.Precision.HIGHEST


def pencil_solve(pencil, blocks, gains):
    harm_rows, columns, radial = pencil.shape
    nblocks, block_rows, _ = blocks.shape
    lines_all = pencil.reshape(harm_rows * columns, nblocks, block_rows)
    product = jnp.einsum('ckj,kij->kci', lines_all, blocks, precision=highest)

    def advance(running, element):
        local_part, gain = element
        updated = local_part + jnp.dot(running, jnp.transpose(gain), precision=highest, preferred_element_type=jnp.float32)
        return updated, updated

    initial = jnp.zeros((harm_rows * columns, block_rows), jnp.float32)
    _, solved = lax.scan(advance, initial, (product, gains))
    return jnp.transpose(solved, (1, 0, 2)).reshape(harm_rows, columns, radial)


def reference(adj_source, face_flux, face_owner, face_cell, block_inverse, carry_gain):
    faces_all = face_owner.shape[0]
    device_ids = jnp.arange(faces_all, dtype=jnp.int32) // F_DEV
    span_ids = device_ids % N_SPAN
    circ_ids = face_owner * CIRC + face_cell // RAD_DEV
    radial_ids = span_ids * RAD_DEV + face_cell % RAD_DEV
    flat_ids = (circ_ids * NRAD + radial_ids).astype(jnp.int32)
    wall_flux = jnp.zeros((HR, NC * NRAD), jnp.float32).at[:, flat_ids].add(face_flux)
    right_side = adj_source + wall_flux.reshape(HR, NC, NRAD)
    blocks = block_inverse.reshape(NRAD // RAD_DEV, RAD_DEV, RAD_DEV)
    gains = carry_gain.reshape(NRAD // RAD_DEV, RAD_DEV, RAD_DEV)
    field = jnp.zeros_like(right_side)
    for sweep_index in range(ITERS):
        neighbours = jnp.roll(field, 1, axis=1) + jnp.roll(field, -1, axis=1)
        field = pencil_solve(right_side + coupling * neighbours, blocks, gains)
    return field
```

```python
import jax
import jax.numpy as jnp
from jax import lax
from jax.experimental import pallas as pl
from jax.experimental.pallas import tpu as pltpu
from jax.sharding import PartitionSpec as P

ITERS = 3
HALO = ITERS - 1

coupling = 0.05
highest = lax.Precision.HIGHEST
VMEM = pl.BlockSpec(memory_space=pltpu.VMEM)
VMEM_LIMIT = 48 * 1024 * 1024


def params():
    return pltpu.CompilerParams(vmem_limit_bytes=VMEM_LIMIT)


def split(x):
    hi = x.astype(jnp.bfloat16)
    return hi, (x - hi.astype(jnp.float32)).astype(jnp.bfloat16)


def pack_kernel(flux, owner, cell, first, last, near, far, diag):
    groups = flux.shape[1] // 128
    odd = lax.rem(lax.axis_index("blade"), 2)
    for message in (near, far, diag):
        for group in range(groups):
            message[group] = flux[:, group * 128 : (group + 1) * 128]
        message[groups] = owner[...].astype(jnp.float32)
        message[groups + 1] = cell[...].astype(jnp.float32)
    rows = first.shape[1]
    for row in range(HALO):
        low = first[:, row, :]
        high = last[:, rows - HALO + row, :]
        near[groups + 2 + row] = jnp.where(odd == 0, high, low)
        diag[groups + 2 + row] = jnp.where(odd == 0, low, high)


def pack(adj_source, face_flux, face_owner, face_cell):
    harm_rows, circum, block_rows = adj_source.shape
    groups = face_owner.shape[0] // 128
    with_halo = jax.ShapeDtypeStruct((groups + 2 + HALO, 8, 128), jnp.float32)
    faces = jax.ShapeDtypeStruct((groups + 2, 8, 128), jnp.float32)
    whole = lambda *shape: pl.BlockSpec(shape, lambda i: (0,) * len(shape))
    last_tile = circum // 8 - 1
    return pl.pallas_call(
        pack_kernel,
        grid=(1,),
        out_shape=(with_halo, faces, with_halo),
        in_specs=[
            whole(*face_flux.shape),
            whole(groups, 128),
            whole(groups, 128),
            pl.BlockSpec((harm_rows, 8, block_rows), lambda i: (0, 0, 0)),
            pl.BlockSpec((harm_rows, 8, block_rows), lambda i: (0, last_tile, 0)),
        ],
        out_specs=(whole(*with_halo.shape), whole(*faces.shape), whole(*with_halo.shape)),
        compiler_params=params(),
        cost_estimate=pl.CostEstimate(flops=0, bytes_accessed=1 << 20, transcendentals=0),
        name="pack",
    )(
        face_flux,
        face_owner.reshape(groups, 128),
        face_cell.reshape(groups, 128),
        adj_source,
        adj_source,
    )


def right_kernel(adj, own, near, far, diag, *rest):
    outs, (hot_rows, weights, acc) = rest[:-3], rest[-3:]
    harm_rows, circum, block_rows = adj.shape
    blades = lax.axis_size("blade")
    blade = lax.axis_index("blade")
    span = lax.axis_index("span")
    total = circum * blades
    groups = own.shape[0] - 2
    rows = hot_rows.shape[0]
    row = lax.broadcasted_iota(jnp.int32, (rows, 128), 0)
    low_at = circum + 8 - HALO
    label = jnp.where(
        row < circum + HALO,
        row,
        jnp.where((row >= low_at) & (row < circum + 8), row - (circum + 8) + total, -1),
    )
    radial = lax.broadcasted_iota(jnp.int32, (block_rows, 128), 0)
    for step, message in enumerate((own, near, far, diag)):
        owner = message[groups].astype(jnp.int32)
        cell = message[groups + 1].astype(jnp.int32)
        place = (owner - blade) * circum + cell // block_rows
        place = jnp.where(place < 0, place + total, place)
        inner = cell % block_rows
        for group in range(groups):
            lanes = slice(group * 128, (group + 1) * 128)
            lanes_low = slice((groups + group) * 128, (groups + group + 1) * 128)
            hot = jnp.where(label == place[group : group + 1, :], 1.0, 0.0).astype(jnp.bfloat16)
            hot_rows[:, lanes] = hot
            hot_rows[:, lanes_low] = hot
            mask = radial == inner[group : group + 1, :]
            flux_hi, flux_lo = split(message[group])
            flux_hi, flux_lo = flux_hi.astype(jnp.float32), flux_lo.astype(jnp.float32)
            for h in range(harm_rows):
                part = slice(h * block_rows, (h + 1) * block_rows)
                weights[part, lanes] = jnp.where(mask, flux_hi[h : h + 1, :], 0.0).astype(
                    jnp.bfloat16
                )
                weights[part, lanes_low] = jnp.where(mask, flux_lo[h : h + 1, :], 0.0).astype(
                    jnp.bfloat16
                )
        product = lax.dot_general(
            hot_rows[...],
            weights[...],
            (((1,), (1,)), ((), ())),
            preferred_element_type=jnp.float32,
        )
        if step == 0:
            acc[...] = product
        else:
            acc[...] += product
    odd = lax.rem(blade, 2)
    above = [
        jnp.where(odd == 0, near[groups + 2 + i], diag[groups + 2 + i]) for i in range(HALO)
    ]
    below = [
        jnp.where(odd == 0, diag[groups + 2 + i], near[groups + 2 + i]) for i in range(HALO)
    ]
    gap = jnp.zeros((8 - 2 * HALO, 128), jnp.float32)
    tiles = jnp.stack(
        [
            jnp.concatenate(
                [v[h : h + 1] for v in above] + [gap] + [v[h : h + 1] for v in below], axis=0
            )
            for h in range(harm_rows)
        ]
    )
    for h in range(harm_rows):
        acc[circum : circum + 8, h * block_rows : (h + 1) * block_rows] += tiles[h]
    for i, out in enumerate(outs):
        h = lax.bitwise_xor(span, i)
        lanes = pl.ds(pl.multiple_of(h * block_rows, block_rows), block_rows)
        out[0:circum, :] = adj[h] + acc[0:circum, lanes]
        out[circum : circum + 8, :] = acc[circum : circum + 8, lanes]


def right_pieces(adj_source, messages):
    harm_rows, circum, block_rows = adj_source.shape
    faces = (messages[0].shape[0] - 2) * 128
    piece = jax.ShapeDtypeStruct((circum + 8, block_rows), jnp.float32)
    return pl.pallas_call(
        right_kernel,
        out_shape=(piece,) * harm_rows,
        in_specs=[VMEM] * 5,
        out_specs=(VMEM,) * harm_rows,
        scratch_shapes=[
            pltpu.VMEM((circum + 16, 2 * faces), jnp.bfloat16),
            pltpu.VMEM((harm_rows * block_rows, 2 * faces), jnp.bfloat16),
            pltpu.VMEM((circum + 16, harm_rows * block_rows), jnp.float32),
        ],
        compiler_params=params(),
        cost_estimate=pl.CostEstimate(
            flops=5_000_000_000, bytes_accessed=3 << 20, transcendentals=0
        ),
        name="right_side",
    )(adj_source, *messages)


def sweep_kernel(*refs):
    count = lax.axis_size("span")
    pieces, (mine, partner) = refs[:count], refs[count : count + 2]
    outs = refs[count + 2 : 2 * count + 2]
    right, weights, solved = refs[2 * count + 2 :]
    span = lax.axis_index("span")
    circum, block_rows = outs[0].shape
    rows = right.shape[1]
    for i in range(count):
        k = lax.bitwise_xor(span, i)
        right[k, 0 : circum + 8, :] = pieces[i][...]
        right[k, circum + 8 : circum + 16, :] = pieces[i][circum : circum + 8, :]
        blocks = (mine, partner)[i % 2]
        for part in range(2):
            hi, lo = split(blocks[i // 2, part * block_rows : (part + 1) * block_rows, :])
            lanes = slice(part * block_rows, (part + 1) * block_rows)
            weights[k, 0:block_rows, lanes] = hi
            weights[k, block_rows : 2 * block_rows, lanes] = lo

    def solve(rhs, below, k):
        rhs_hi, rhs_lo = split(rhs)
        below_hi, below_lo = split(below)
        left = jnp.concatenate(
            [
                jnp.concatenate([rhs_hi, below_hi], axis=1),
                jnp.concatenate([rhs_lo, below_lo], axis=1),
            ],
            axis=0,
        )
        product = lax.dot_general(
            left, weights[k], (((1,), (1,)), ((), ())), preferred_element_type=jnp.float32
        )
        high, low = product[:rows], product[rows:]
        return (high[:, :block_rows] + (low[:, :block_rows] + high[:, block_rows:])) + low[
            :, block_rows:
        ]

    fields = [jnp.zeros((rows, block_rows), jnp.float32)] * ITERS
    for k in range(count):
        rhs = right[k]
        base = rhs
        for sweep in range(ITERS):
            if sweep > 0:
                field = fields[sweep - 1]
                around = pltpu.roll(field, 1, 0) + pltpu.roll(field, rows - 1, 0)
                rhs = base + coupling * around
            fields[sweep] = solve(rhs, fields[sweep], k)
        solved[k] = fields[-1][:circum]
    for i in range(count):
        outs[i][...] = solved[lax.bitwise_xor(span, i)]


def sweep_pieces(pieces, mine, partner):
    count = len(pieces)
    rows, block_rows = pieces[0].shape
    circum = rows - 8
    piece = jax.ShapeDtypeStruct((circum, block_rows), jnp.float32)
    return pl.pallas_call(
        sweep_kernel,
        out_shape=(piece,) * count,
        in_specs=[VMEM] * (count + 2),
        out_specs=(VMEM,) * count,
        scratch_shapes=[
            pltpu.VMEM((count, circum + 16, block_rows), jnp.float32),
            pltpu.VMEM((count, 2 * block_rows, 2 * block_rows), jnp.bfloat16),
            pltpu.VMEM((count, circum, block_rows), jnp.float32),
        ],
        compiler_params=params(),
        cost_estimate=pl.CostEstimate(
            flops=2_000_000_000, bytes_accessed=3 << 20, transcendentals=0
        ),
        name="sweeps",
    )(*pieces, mine, partner)


def place_kernel(*refs):
    pieces, out = refs[:-1], refs[-1]
    span = lax.axis_index("span")
    for i, piece in enumerate(pieces):
        out[lax.bitwise_xor(span, i)] = piece[...]


def place(pieces):
    return pl.pallas_call(
        place_kernel,
        out_shape=jax.ShapeDtypeStruct((len(pieces), *pieces[0].shape), jnp.float32),
        in_specs=[VMEM] * len(pieces),
        out_specs=VMEM,
        compiler_params=params(),
        cost_estimate=pl.CostEstimate(flops=0, bytes_accessed=2 << 20, transcendentals=0),
        name="place",
    )(*pieces)


def exchange(array, axis, bits):
    count = lax.axis_size(axis)
    return lax.ppermute(array, axis, [(i, i ^ bits) for i in range(count)])


def by_harmonics(adj_source, face_flux, face_owner, face_cell, block_inverse, carry_gain):
    count = lax.axis_size("span")
    near, far, diag = pack(adj_source, face_flux, face_owner, face_cell)
    operators = jnp.concatenate([block_inverse, carry_gain], axis=0)
    messages = [
        far,
        exchange(near, "blade", 1),
        exchange(far, "blade", 2),
        exchange(diag, "blade", 3),
    ]
    mine = jnp.stack(
        [operators] + [exchange(operators, "span", bits) for bits in range(2, count, 2)]
    )
    partner = exchange(mine, "span", 1)
    pieces = right_pieces(adj_source, messages)
    pieces = [p if i == 0 else exchange(p, "span", i) for i, p in enumerate(pieces)]
    pieces = sweep_pieces(pieces, mine, partner)
    pieces = [p if i == 0 else exchange(p, "span", i) for i, p in enumerate(pieces)]
    return place(pieces)

def extended(block, sides, width):
    for axis, dim in sides:
        count = lax.axis_size(axis)
        forward = [(i, i + 1) for i in range(count - 1)]
        forward.append((count - 1, 0))
        backward = [(target, source) for source, target in forward]
        low = lax.ppermute(
            lax.slice_in_dim(block, block.shape[dim] - width, None, axis=dim), axis, forward
        )
        high = lax.ppermute(lax.slice_in_dim(block, 0, width, axis=dim), axis, backward)
        block = jnp.concatenate([low, block, high], axis=dim)
    return block


def pencil_solve(pencil, blocks, gains):
    harm_rows, columns, radial = pencil.shape
    nblocks, block_rows, _ = blocks.shape
    lines_all = pencil.reshape(harm_rows * columns, nblocks, block_rows)
    product = jnp.einsum("ckj,kij->kci", lines_all, blocks, precision=highest)

    def advance(running, element):
        local_part, gain = element
        updated = local_part + lax.dot_general(
            running,
            gain,
            (((1,), (1,)), ((), ())),
            precision=highest,
            preferred_element_type=jnp.float32,
        )
        return (updated, updated)

    initial = jnp.zeros((harm_rows * columns, block_rows), jnp.float32)
    _, solved = lax.scan(advance, initial, (product, gains))
    return jnp.transpose(solved, (1, 0, 2)).reshape(harm_rows, columns, radial)


def row_rhs(right_side, field):
    widened = extended(field, (("blade", 1),), 1)
    return right_side + coupling * (widened[:, :-2, :] + widened[:, 2:, :])


def by_lines(adj_source, face_flux, face_owner, face_cell, block_inverse, carry_gain):
    harm_rows, circum, block_rows = adj_source.shape
    blades = lax.axis_size("blade")
    faces_dev = face_owner.shape[0]
    capacity = faces_dev // 2
    onehot = (face_owner[:, None] == jnp.arange(blades, dtype=jnp.int32)[None, :]).astype(jnp.int32)
    rank_in = jnp.sum((jnp.cumsum(onehot, axis=0) - 1) * onehot, axis=1)
    slot_ids = face_owner * capacity + rank_in
    send_flux = (
        jnp.zeros((harm_rows, blades * capacity), jnp.float32)
        .at[:, slot_ids]
        .set(face_flux)
        .reshape(harm_rows, blades, capacity)
    )
    send_cell = (
        jnp.zeros((blades * capacity,), jnp.int32)
        .at[slot_ids]
        .set(face_cell)
        .reshape(1, blades, capacity)
    )
    fluxes, cell_ids = (
        lax.all_to_all(send_flux, "blade", split_axis=1, concat_axis=1, tiled=True),
        lax.all_to_all(send_cell, "blade", split_axis=1, concat_axis=1, tiled=True),
    )
    fluxes = fluxes.reshape(harm_rows, blades * capacity)
    cell_ids = cell_ids.reshape(blades * capacity)
    wall_flux = jnp.zeros((harm_rows, circum * block_rows), jnp.float32).at[:, cell_ids].add(fluxes)
    right_side = adj_source + wall_flux.reshape(harm_rows, circum, block_rows)
    inverses, couplings = (
        lax.all_gather(block_inverse, "span", axis=0, tiled=True),
        lax.all_gather(carry_gain, "span", axis=0, tiled=True),
    )
    blocks = inverses.reshape(-1, block_rows, block_rows)
    gains = couplings.reshape(-1, block_rows, block_rows)

    def transposed(rhs_rows):
        pencil = lax.all_to_all(rhs_rows, "span", split_axis=1, concat_axis=2, tiled=True)
        return lax.all_to_all(
            pencil_solve(pencil, blocks, gains), "span", split_axis=2, concat_axis=1, tiled=True
        )

    field = transposed(right_side)
    for sweep_index in range(1, ITERS):
        field = transposed(row_rhs(right_side, field))
    return field


def body(adj_source, *others):
    harm_rows, circum, block_rows = adj_source.shape
    if lax.axis_size("span") == harm_rows == 8 and lax.axis_size("blade") == 4:
        return by_harmonics(adj_source, *others)
    return by_lines(adj_source, *others)


def solution(mesh):
    in_specs = (
        P(None, "blade", "span"),
        P(None, ("blade", "span")),
        P(("blade", "span")),
        P(("blade", "span")),
        P("span", None),
        P("span", None),
    )
    out_specs = P(None, "blade", "span")
    return jax.shard_map(body, mesh=mesh, in_specs=in_specs, out_specs=out_specs, check_vma=False)
```

```python
import functools

import jax
import jax.numpy as jnp
from jax import lax
from jax.experimental import pallas as pl
from jax.experimental.pallas import tpu as pltpu
from jax.sharding import PartitionSpec as P

ITERS = 3
HALO = ITERS - 1

coupling = 0.05
highest = lax.Precision.HIGHEST
VMEM = pl.BlockSpec(memory_space=pltpu.VMEM)
ANY = pl.BlockSpec(memory_space=pl.ANY)
HBM = pl.BlockSpec(memory_space=pltpu.HBM)
F32 = jnp.float32
BF16 = jnp.bfloat16


def call(kernel, outs, ins, scratch, flops, name, out_specs=None, vmem=24):
    shapes = tuple(jax.ShapeDtypeStruct(shape, dtype) for shape, dtype in outs)
    return pl.pallas_call(
        kernel,
        out_shape=shapes,
        in_specs=ins,
        out_specs=out_specs or (VMEM,) * len(outs),
        scratch_shapes=scratch,
        compiler_params=pltpu.CompilerParams(vmem_limit_bytes=vmem * 1024 * 1024),
        cost_estimate=pl.CostEstimate(flops=flops, bytes_accessed=1 << 20, transcendentals=0),
        name=name,
    )


def split(x):
    hi = x.astype(BF16)
    return hi, (x - hi.astype(F32)).astype(BF16)


def peer(i):
    return lax.bitwise_xor(lax.axis_index("span"), i)


def pack_kernel(flux, owner, cell, adj, inverse, gain, near, far, diag, operators, *scratch):
    faces, owners, cells, first, last, sems = scratch
    groups, circum, block_rows = owner.shape[0], adj.shape[1], inverse.shape[0]
    odd = lax.rem(lax.axis_index("blade"), 2)
    pairs = (
        (flux, faces),
        (owner, owners),
        (cell, cells),
        (adj.at[:, 0:8, :], first),
        (adj.at[:, circum - 8 : circum, :], last),
        (inverse, operators.at[0:block_rows, :]),
        (gain, operators.at[block_rows : 2 * block_rows, :]),
    )
    copies = [pltpu.make_async_copy(a, b, sems.at[i]) for i, (a, b) in enumerate(pairs)]
    for copy in copies:
        copy.start()
    for copy in copies:
        copy.wait()
    for message in (near, far, diag):
        for group in range(groups):
            message[group] = faces[:, group * 128 : (group + 1) * 128]
        message[groups] = owners[...].astype(F32)
        message[groups + 1] = cells[...].astype(F32)
    for row in range(HALO):
        low = first[:, row, :]
        high = last[:, 8 - HALO + row, :]
        near[groups + 2 + row] = jnp.where(odd == 0, high, low)
        diag[groups + 2 + row] = jnp.where(odd == 0, low, high)


def pack(adj_source, face_flux, face_owner, face_cell, block_inverse, carry_gain):
    groups = face_owner.shape[0] // 128
    block_rows = adj_source.shape[2]
    with_halo = ((groups + 2 + HALO, 8, 128), F32)
    faces = ((groups + 2, 8, 128), F32)
    edge = pltpu.VMEM((8, 8, block_rows), F32)
    return call(
        pack_kernel,
        (with_halo, faces, with_halo, ((2 * block_rows, block_rows), F32)),
        [HBM] * 6,
        [
            pltpu.VMEM(face_flux.shape, F32),
            pltpu.VMEM((groups, 128), jnp.int32),
            pltpu.VMEM((groups, 128), jnp.int32),
            edge,
            edge,
            pltpu.SemaphoreType.DMA((7,)),
        ],
        0,
        "pack",
        vmem=60,
    )(
        face_flux,
        face_owner.reshape(groups, 128),
        face_cell.reshape(groups, 128),
        adj_source,
        block_inverse,
        carry_gain,
    )


def face_product(message, hot_rows, weights, harmonics, circum, block_rows):
    blades = lax.axis_size("blade")
    blade = lax.axis_index("blade")
    total = circum * blades
    groups = weights.shape[1] // 256
    rows = hot_rows.shape[0]
    row = lax.broadcasted_iota(jnp.int32, (rows, 128), 0)
    label = jnp.where(
        row < circum + HALO,
        row,
        jnp.where(
            (row >= circum + 8 - HALO) & (row < circum + 8), row - (circum + 8) + total, -1
        ),
    )
    radial = lax.broadcasted_iota(jnp.int32, (block_rows, 128), 0)
    owner = message[groups].astype(jnp.int32)
    cell = message[groups + 1].astype(jnp.int32)
    place = (owner - blade) * circum + cell // block_rows
    place = jnp.where(place < 0, place + total, place)
    inner = cell % block_rows
    for group in range(groups):
        lanes = slice(group * 128, (group + 1) * 128)
        lanes_low = slice((groups + group) * 128, (groups + group + 1) * 128)
        hot = jnp.where(label == place[group : group + 1, :], 1.0, 0.0).astype(BF16)
        hot_rows[:, lanes] = hot
        hot_rows[:, lanes_low] = hot
        hit = jnp.where(radial == inner[group : group + 1, :], 1.0, 0.0).astype(BF16)
        hit = hit.reshape(block_rows // 16, 16, 128)
        for at, h in enumerate(harmonics):
            flux = jnp.broadcast_to(message[group, pl.ds(h, 1), :], (16, 128))
            flux_hi, flux_lo = split(flux)
            part = slice(at * block_rows, (at + 1) * block_rows)
            weights[part, lanes] = (hit * flux_hi[None]).reshape(block_rows, 128)
            weights[part, lanes_low] = (hit * flux_lo[None]).reshape(block_rows, 128)
    return lax.dot_general(
        hot_rows[...], weights[...], (((1,), (1,)), ((), ())), preferred_element_type=F32
    )


def own_faces_kernel(own, acc, hot_rows, weights):
    block_rows = 128
    circum = acc.shape[0] - 16
    harmonics = range(acc.shape[1] // block_rows)
    acc[...] = face_product(own, hot_rows, weights, harmonics, circum, block_rows)


def own_faces(own, harm_rows, circum):
    faces = (own.shape[0] - 2) * 128
    rows, lanes = circum + 16, harm_rows * 128
    return call(
        own_faces_kernel,
        (((rows, lanes), F32),),
        [VMEM],
        [pltpu.VMEM((rows, 2 * faces), BF16), pltpu.VMEM((lanes, 2 * faces), BF16)],
        1_200_000_000,
        "own_faces",
    )(own)[0]


def right_kernel(peers, adj, start, near, far, diag, *rest):
    count = len(peers)
    *outs, hot_rows, weights, acc, source, sems = rest
    del outs[: len(outs) - count - 1]
    outs[count][...] = jnp.zeros_like(outs[count])
    _, circum, block_rows = adj.shape
    copies = [
        pltpu.make_async_copy(adj.at[peer(i)], source.at[at], sems.at[at])
        for at, i in enumerate(peers)
    ]
    for copy in copies:
        copy.start()
    groups = weights.shape[2] // 256
    odd = lax.rem(lax.axis_index("blade"), 2)
    harmonics = [peer(i) for i in peers]
    for at, h in enumerate(harmonics):
        lanes = pl.ds(pl.multiple_of(h * block_rows, block_rows), block_rows)
        acc[:, at * block_rows : (at + 1) * block_rows] = start[:, lanes]
    for step, message in enumerate((near, far, diag)):
        product = face_product(
            message, hot_rows.at[step], weights.at[step], harmonics, circum, block_rows
        )
        acc[...] += product
    gap = jnp.zeros((8 - 2 * HALO, 128), F32)
    for copy in copies:
        copy.wait()
    for at, (i, out) in enumerate(zip(peers, outs[:count], strict=True)):
        row = pl.ds(peer(i), 1)
        one = [near[groups + 2 + j, row, :] for j in range(HALO)]
        three = [diag[groups + 2 + j, row, :] for j in range(HALO)]
        above = [jnp.where(odd == 0, a, b) for a, b in zip(one, three, strict=True)]
        below = [jnp.where(odd == 0, b, a) for a, b in zip(one, three, strict=True)]
        part = slice(at * block_rows, (at + 1) * block_rows)
        out[0:circum, :] = source[at] + acc[0:circum, part]
        out[circum : circum + 8, :] = acc[circum : circum + 8, part] + jnp.concatenate(
            above + [gap] + below, axis=0
        )


def right_pieces(peers, adj_source, start, messages, after, name):
    _, circum, block_rows = adj_source.shape
    count = len(peers)
    faces = (messages[1].shape[0] - 2) * 128
    rows = circum + 16
    return call(
        functools.partial(right_kernel, peers),
        (((circum + 8, block_rows), F32),) * count + (((8, 128), F32),),
        [HBM] + [VMEM] * 4 + [ANY] * len(after),
        [
            pltpu.VMEM((3, rows, 2 * faces), BF16),
            pltpu.VMEM((3, count * block_rows, 2 * faces), BF16),
            pltpu.VMEM((rows, count * block_rows), F32),
            pltpu.VMEM((count, circum, block_rows), F32),
            pltpu.SemaphoreType.DMA((count,)),
        ],
        1_800_000_000,
        name,
    )(adj_source, start, *messages, *after)


def solve_half(pieces, weights, first, fields, right, solved):
    half = len(pieces)
    rows, block_rows = right.shape[1:]
    circum = rows - 16
    for i, piece in enumerate(pieces):
        k = lax.rem(peer(i), half)
        right[k, 0 : circum + 8, :] = piece[...]
        right[k, circum + 8 : rows, :] = piece[circum : circum + 8, :]

    def solve(rhs, below, k):
        rhs_hi, rhs_lo = split(rhs)
        below_hi, below_lo = split(below)
        left = jnp.concatenate(
            [
                jnp.concatenate([rhs_hi, below_hi], axis=1),
                jnp.concatenate([rhs_lo, below_lo], axis=1),
            ],
            axis=0,
        )
        product = lax.dot_general(
            left, weights[first + k], (((1,), (1,)), ((), ())), preferred_element_type=F32
        )
        high, low = product[:rows], product[rows:]
        cross = low[:, :block_rows] + high[:, block_rows:]
        return (high[:, :block_rows] + cross) + low[:, block_rows:]

    fields = list(fields)
    for k in range(half):
        base = rhs = right[k]
        for sweep in range(ITERS):
            if sweep > 0:
                field = fields[sweep - 1]
                around = pltpu.roll(field, 1, 0) + pltpu.roll(field, rows - 1, 0)
                rhs = base + coupling * around
            fields[sweep] = solve(rhs, fields[sweep], k)
        solved[k] = fields[-1][:circum]
    return fields


def stack_kernel(*refs):
    *pieces, _, out = refs
    for i, piece in enumerate(pieces):
        out[i] = piece[...]


def operators_kernel(mine, partner, weights):
    block_rows = mine.shape[2]
    for i in range(weights.shape[0]):
        k = peer(i)
        source = (mine, partner)[i % 2]
        for matrix in range(2):
            part = slice(matrix * block_rows, (matrix + 1) * block_rows)
            hi, lo = split(source[i // 2, part, :])
            weights[k, 0:block_rows, part] = hi
            weights[k, block_rows : 2 * block_rows, part] = lo


def lower_kernel(half, *refs):
    *rest, weights, state, solved, right = refs
    pieces = rest[len(rest) - half :]
    upper = lax.axis_index("span") // half
    zero = jnp.zeros(state.shape[1:], F32)

    @pl.when(upper == 0)
    def _():
        for sweep, field in enumerate(
            solve_half(pieces, weights, 0, [zero] * ITERS, right, solved)
        ):
            state[sweep] = field

    @pl.when(upper != 0)
    def _():
        for sweep in range(ITERS):
            state[sweep] = zero


def far_kernel(half, *refs):
    pieces, (weights, state) = refs[:half], refs[half : half + 2]
    outs = refs[half + 2 : 2 * half + 2]
    after, right, solved = refs[2 * half + 2 :]
    upper = lax.axis_index("span") // half
    fields = solve_half(
        pieces, weights, (1 - upper) * half, [state[i] for i in range(ITERS)], right, solved
    )
    for i, out in enumerate(outs):
        out[...] = solved[lax.rem(peer(i), half)]
    for sweep, field in enumerate(fields):
        after[sweep] = field


def upper_kernel(half, *refs):
    pieces, (weights, state, done) = refs[:half], refs[half : half + 3]
    outs = refs[half + 3 : 2 * half + 3]
    right, solved = refs[2 * half + 3 :]
    upper = lax.axis_index("span") // half

    @pl.when(upper == 0)
    def _():
        for i, out in enumerate(outs):
            out[...] = done[lax.rem(peer(i), half)]

    @pl.when(upper != 0)
    def _():
        solve_half(pieces, weights, half, [state[i] for i in range(ITERS)], right, solved)
        for i, out in enumerate(outs):
            out[...] = solved[lax.rem(peer(i), half)]


def place_kernel(peers, *refs):
    *pieces, out, sems = refs
    copies = [
        pltpu.make_async_copy(piece, out.at[peer(i)], sems.at[i])
        for i, piece in zip(peers, pieces, strict=True)
    ]
    for copy in copies:
        copy.start()
    for copy in copies:
        copy.wait()


def exchange(array, axis, bits):
    count = lax.axis_size(axis)
    return lax.ppermute(array, axis, [(i, i ^ bits) for i in range(count)])


def by_harmonics(adj_source, face_flux, face_owner, face_cell, block_inverse, carry_gain):
    harm_rows, circum, block_rows = adj_source.shape
    count = lax.axis_size("span")
    half = count // 2
    near, far, diag, operators = pack(
        adj_source, face_flux, face_owner, face_cell, block_inverse, carry_gain
    )
    messages = [
        exchange(near, "blade", 1),
        exchange(far, "blade", 2),
        exchange(diag, "blade", 3),
    ]
    start = own_faces(far, harm_rows, circum)
    operators = [operators] + [exchange(operators, "span", bits) for bits in range(2, count, 2)]
    far_peers, near_peers = range(half, count), range(half)
    *far_right, token = right_pieces(far_peers, adj_source, start, messages, [], "right_far")
    far_right = [exchange(p, "span", i) for p, i in zip(far_right, far_peers, strict=True)]
    mine = call(
        stack_kernel,
        (((half, *operators[0].shape), F32),),
        [VMEM] * half + [ANY],
        [],
        0,
        "stack",
    )(*operators, token)[0]
    partner = exchange(mine, "span", 1)
    weights = call(
        operators_kernel,
        (((count, 2 * block_rows, 2 * block_rows), BF16),),
        [VMEM] * 2,
        [],
        0,
        "operators",
    )(mine, partner)[0]
    *near_right, _ = right_pieces(near_peers, adj_source, start, messages, [token, weights], "right_near")
    near_right = [p if i == 0 else exchange(p, "span", i) for i, p in enumerate(near_right)]

    rows = circum + 16
    right = pltpu.VMEM((half, rows, block_rows), F32)
    solved = pltpu.VMEM((half, circum, block_rows), F32)
    state_shape = ((ITERS, rows, block_rows), F32)
    piece = ((circum, block_rows), F32)
    state, done = call(
        functools.partial(lower_kernel, half),
        (state_shape, ((half, circum, block_rows), F32)),
        [ANY] * 3 + [VMEM] * (half + 1),
        [right],
        1_000_000_000,
        "sweeps_lower",
    )(*far_right[:3], *near_right, weights)
    *far_solved, state = call(
        functools.partial(far_kernel, half),
        (piece,) * half + (state_shape,),
        [VMEM] * (half + 2),
        [right, solved],
        1_000_000_000,
        "sweeps_far",
    )(*far_right, weights, state)
    far_solved = [exchange(p, "span", i) for p, i in zip(far_solved, far_peers, strict=True)]
    near_solved = call(
        functools.partial(upper_kernel, half),
        (piece,) * half,
        [VMEM] * (half + 3),
        [right, solved],
        1_000_000_000,
        "sweeps_upper",
    )(*near_right, weights, state, done)
    near_solved = [p if i == 0 else exchange(p, "span", i) for i, p in enumerate(near_solved)]
    return call(
        functools.partial(place_kernel, (*far_peers, *near_peers)),
        (((count, circum, block_rows), F32),),
        [ANY] * count,
        [pltpu.SemaphoreType.DMA((count,))],
        0,
        "place",
        out_specs=(ANY,),
    )(*far_solved, *near_solved)[0]


def extended(block, sides, width):
    for axis, dim in sides:
        count = lax.axis_size(axis)
        forward = [(i, i + 1) for i in range(count - 1)]
        forward.append((count - 1, 0))
        backward = [(target, source) for source, target in forward]
        low = lax.ppermute(
            lax.slice_in_dim(block, block.shape[dim] - width, None, axis=dim), axis, forward
        )
        high = lax.ppermute(lax.slice_in_dim(block, 0, width, axis=dim), axis, backward)
        block = jnp.concatenate([low, block, high], axis=dim)
    return block


def pencil_solve(pencil, blocks, gains):
    harm_rows, columns, radial = pencil.shape
    nblocks, block_rows, _ = blocks.shape
    lines_all = pencil.reshape(harm_rows * columns, nblocks, block_rows)
    product = jnp.einsum("ckj,kij->kci", lines_all, blocks, precision=highest)

    def advance(running, element):
        local_part, gain = element
        updated = local_part + lax.dot_general(
            running,
            gain,
            (((1,), (1,)), ((), ())),
            precision=highest,
            preferred_element_type=jnp.float32,
        )
        return (updated, updated)

    initial = jnp.zeros((harm_rows * columns, block_rows), jnp.float32)
    _, solved = lax.scan(advance, initial, (product, gains))
    return jnp.transpose(solved, (1, 0, 2)).reshape(harm_rows, columns, radial)


def row_rhs(right_side, field):
    widened = extended(field, (("blade", 1),), 1)
    return right_side + coupling * (widened[:, :-2, :] + widened[:, 2:, :])


def by_lines(adj_source, face_flux, face_owner, face_cell, block_inverse, carry_gain):
    harm_rows, circum, block_rows = adj_source.shape
    blades = lax.axis_size("blade")
    faces_dev = face_owner.shape[0]
    capacity = faces_dev // 2
    onehot = (face_owner[:, None] == jnp.arange(blades, dtype=jnp.int32)[None, :]).astype(jnp.int32)
    rank_in = jnp.sum((jnp.cumsum(onehot, axis=0) - 1) * onehot, axis=1)
    slot_ids = face_owner * capacity + rank_in
    send_flux = (
        jnp.zeros((harm_rows, blades * capacity), jnp.float32)
        .at[:, slot_ids]
        .set(face_flux)
        .reshape(harm_rows, blades, capacity)
    )
    send_cell = (
        jnp.zeros((blades * capacity,), jnp.int32)
        .at[slot_ids]
        .set(face_cell)
        .reshape(1, blades, capacity)
    )
    fluxes, cell_ids = (
        lax.all_to_all(send_flux, "blade", split_axis=1, concat_axis=1, tiled=True),
        lax.all_to_all(send_cell, "blade", split_axis=1, concat_axis=1, tiled=True),
    )
    fluxes = fluxes.reshape(harm_rows, blades * capacity)
    cell_ids = cell_ids.reshape(blades * capacity)
    wall_flux = jnp.zeros((harm_rows, circum * block_rows), jnp.float32).at[:, cell_ids].add(fluxes)
    right_side = adj_source + wall_flux.reshape(harm_rows, circum, block_rows)
    inverses, couplings = (
        lax.all_gather(block_inverse, "span", axis=0, tiled=True),
        lax.all_gather(carry_gain, "span", axis=0, tiled=True),
    )
    blocks = inverses.reshape(-1, block_rows, block_rows)
    gains = couplings.reshape(-1, block_rows, block_rows)

    def transposed(rhs_rows):
        pencil = lax.all_to_all(rhs_rows, "span", split_axis=1, concat_axis=2, tiled=True)
        return lax.all_to_all(
            pencil_solve(pencil, blocks, gains), "span", split_axis=2, concat_axis=1, tiled=True
        )

    field = transposed(right_side)
    for sweep_index in range(1, ITERS):
        field = transposed(row_rhs(right_side, field))
    return field


def body(adj_source, *others):
    harm_rows, circum, block_rows = adj_source.shape
    if lax.axis_size("span") == harm_rows == 8 and lax.axis_size("blade") == 4:
        return by_harmonics(adj_source, *others)
    return by_lines(adj_source, *others)


def solution(mesh):
    in_specs = (
        P(None, "blade", "span"),
        P(None, ("blade", "span")),
        P(("blade", "span")),
        P(("blade", "span")),
        P("span", None),
        P("span", None),
    )
    out_specs = P(None, "blade", "span")
    return jax.shard_map(body, mesh=mesh, in_specs=in_specs, out_specs=out_specs, check_vma=False)
```

```python
import functools

import jax
import jax.numpy as jnp
from jax import lax
from jax.experimental import pallas as pl
from jax.experimental.pallas import tpu as pltpu
from jax.sharding import PartitionSpec as P

ITERS = 3
HALO = ITERS - 1

coupling = 0.05
highest = lax.Precision.HIGHEST
VMEM = pl.BlockSpec(memory_space=pltpu.VMEM)
ANY = pl.BlockSpec(memory_space=pl.ANY)
HBM = pl.BlockSpec(memory_space=pltpu.HBM)
F32 = jnp.float32
BF16 = jnp.bfloat16


def call(kernel, outs, ins, scratch, flops, name, out_specs=None, vmem=24):
    shapes = tuple(jax.ShapeDtypeStruct(shape, dtype) for shape, dtype in outs)
    return pl.pallas_call(
        kernel,
        out_shape=shapes,
        in_specs=ins,
        out_specs=out_specs or (VMEM,) * len(outs),
        scratch_shapes=scratch,
        compiler_params=pltpu.CompilerParams(vmem_limit_bytes=vmem * 1024 * 1024),
        cost_estimate=pl.CostEstimate(flops=flops, bytes_accessed=1 << 20, transcendentals=0),
        name=name,
    )


def split(x):
    hi = x.astype(BF16)
    return hi, (x - hi.astype(F32)).astype(BF16)


def peer(i):
    return lax.bitwise_xor(lax.axis_index("span"), i)


def pack_kernel(flux, owner, cell, adj, inverse, gain, near, far, diag, operators, *scratch):
    faces, owners, cells, first, last, sems = scratch
    groups, circum, block_rows = owner.shape[0], adj.shape[1], inverse.shape[0]
    odd = lax.rem(lax.axis_index("blade"), 2)
    pairs = (
        (flux, faces),
        (owner, owners),
        (cell, cells),
        (adj.at[:, 0:8, :], first),
        (adj.at[:, circum - 8 : circum, :], last),
        (inverse, operators.at[0:block_rows, :]),
        (gain, operators.at[block_rows : 2 * block_rows, :]),
    )
    copies = [pltpu.make_async_copy(a, b, sems.at[i]) for i, (a, b) in enumerate(pairs)]
    for copy in copies:
        copy.start()
    for copy in copies:
        copy.wait()
    for message in (near, far, diag):
        for group in range(groups):
            message[group] = faces[:, group * 128 : (group + 1) * 128]
        message[groups] = owners[...].astype(F32)
        message[groups + 1] = cells[...].astype(F32)
    for row in range(HALO):
        low = first[:, row, :]
        high = last[:, 8 - HALO + row, :]
        near[groups + 2 + row] = jnp.where(odd == 0, high, low)
        diag[groups + 2 + row] = jnp.where(odd == 0, low, high)


def pack(adj_source, face_flux, face_owner, face_cell, block_inverse, carry_gain):
    groups = face_owner.shape[0] // 128
    block_rows = adj_source.shape[2]
    with_halo = ((groups + 2 + HALO, 8, 128), F32)
    faces = ((groups + 2, 8, 128), F32)
    edge = pltpu.VMEM((8, 8, block_rows), F32)
    return call(
        pack_kernel,
        (with_halo, faces, with_halo, ((2 * block_rows, block_rows), F32)),
        [HBM] * 6,
        [
            pltpu.VMEM(face_flux.shape, F32),
            pltpu.VMEM((groups, 128), jnp.int32),
            pltpu.VMEM((groups, 128), jnp.int32),
            edge,
            edge,
            pltpu.SemaphoreType.DMA((7,)),
        ],
        0,
        "pack",
        vmem=60,
    )(
        face_flux,
        face_owner.reshape(groups, 128),
        face_cell.reshape(groups, 128),
        adj_source,
        block_inverse,
        carry_gain,
    )


def face_product(message, hot_rows, weights, harmonics, circum, block_rows):
    blades = lax.axis_size("blade")
    blade = lax.axis_index("blade")
    total = circum * blades
    groups = weights.shape[1] // 256
    rows = hot_rows.shape[0]
    row = lax.broadcasted_iota(jnp.int32, (rows, 128), 0)
    label = jnp.where(
        row < circum + HALO,
        row,
        jnp.where(
            (row >= circum + 8 - HALO) & (row < circum + 8), row - (circum + 8) + total, -1
        ),
    )
    radial = lax.broadcasted_iota(jnp.int32, (block_rows, 128), 0)
    owner = message[groups].astype(jnp.int32)
    cell = message[groups + 1].astype(jnp.int32)
    place = (owner - blade) * circum + cell // block_rows
    place = jnp.where(place < 0, place + total, place)
    inner = cell % block_rows
    for group in range(groups):
        lanes = slice(group * 128, (group + 1) * 128)
        lanes_low = slice((groups + group) * 128, (groups + group + 1) * 128)
        hot = jnp.where(label == place[group : group + 1, :], 1.0, 0.0).astype(BF16)
        hot_rows[:, lanes] = hot
        hot_rows[:, lanes_low] = hot
        hit = jnp.where(radial == inner[group : group + 1, :], 1.0, 0.0).astype(BF16)
        hit = hit.reshape(block_rows // 16, 16, 128)
        for at, h in enumerate(harmonics):
            flux = jnp.broadcast_to(message[group, pl.ds(h, 1), :], (16, 128))
            flux_hi, flux_lo = split(flux)
            part = slice(at * block_rows, (at + 1) * block_rows)
            weights[part, lanes] = (hit * flux_hi[None]).reshape(block_rows, 128)
            weights[part, lanes_low] = (hit * flux_lo[None]).reshape(block_rows, 128)
    return lax.dot_general(
        hot_rows[...], weights[...], (((1,), (1,)), ((), ())), preferred_element_type=F32
    )


def own_faces_kernel(peers, own, acc, hot_rows, weights):
    block_rows = 128
    circum = acc.shape[0] - 16
    harmonics = [peer(i) for i in peers]
    acc[...] = face_product(own, hot_rows, weights, harmonics, circum, block_rows)


def own_faces(peers, own, circum):
    faces = (own.shape[0] - 2) * 128
    rows, lanes = circum + 16, len(peers) * 128
    return call(
        functools.partial(own_faces_kernel, peers),
        (((rows, lanes), F32),),
        [VMEM],
        [pltpu.VMEM((rows, 2 * faces), BF16), pltpu.VMEM((lanes, 2 * faces), BF16)],
        600_000_000,
        "own_faces",
    )(own)[0]


def right_kernel(peers, own, adj, start, near, far, diag, *rest):
    count = len(peers)
    *outs, hot_rows, weights, acc, source, sems = rest
    del outs[: len(outs) - count - 1]
    outs[count][...] = jnp.zeros_like(outs[count])
    _, circum, block_rows = adj.shape
    copies = [
        pltpu.make_async_copy(adj.at[peer(i)], source.at[at], sems.at[at])
        for at, i in enumerate(peers)
    ]
    for copy in copies:
        copy.start()
    groups = weights.shape[2] // 256
    odd = lax.rem(lax.axis_index("blade"), 2)
    harmonics = [peer(i) for i in peers]
    messages = (near, far, diag)
    if own:
        messages = (start, *messages)
    else:
        acc[...] = start[...]
    for step, message in enumerate(messages):
        product = face_product(
            message, hot_rows.at[step], weights.at[step], harmonics, circum, block_rows
        )
        if own and step == 0:
            acc[...] = product
        else:
            acc[...] += product
    gap = jnp.zeros((8 - 2 * HALO, 128), F32)
    for copy in copies:
        copy.wait()
    for at, (i, out) in enumerate(zip(peers, outs[:count], strict=True)):
        row = pl.ds(peer(i), 1)
        one = [near[groups + 2 + j, row, :] for j in range(HALO)]
        three = [diag[groups + 2 + j, row, :] for j in range(HALO)]
        above = [jnp.where(odd == 0, a, b) for a, b in zip(one, three, strict=True)]
        below = [jnp.where(odd == 0, b, a) for a, b in zip(one, three, strict=True)]
        part = slice(at * block_rows, (at + 1) * block_rows)
        out[0:circum, :] = source[at] + acc[0:circum, part]
        out[circum : circum + 8, :] = acc[circum : circum + 8, part] + jnp.concatenate(
            above + [gap] + below, axis=0
        )


def right_pieces(peers, own, adj_source, start, messages, after, name):
    _, circum, block_rows = adj_source.shape
    count = len(peers)
    faces = (messages[1].shape[0] - 2) * 128
    rows = circum + 16
    return call(
        functools.partial(right_kernel, peers, own),
        (((circum + 8, block_rows), F32),) * count + (((8, 128), F32),),
        [HBM] + [VMEM] * 4 + [ANY] * len(after),
        [
            pltpu.VMEM((3 + own, rows, 2 * faces), BF16),
            pltpu.VMEM((3 + own, count * block_rows, 2 * faces), BF16),
            pltpu.VMEM((rows, count * block_rows), F32),
            pltpu.VMEM((count, circum, block_rows), F32),
            pltpu.SemaphoreType.DMA((count,)),
        ],
        1_800_000_000,
        name,
    )(adj_source, start, *messages, *after)


def solve_half(pieces, weights, first, fields, right, solved):
    half = len(pieces)
    rows, block_rows = right.shape[1:]
    circum = rows - 16
    for i, piece in enumerate(pieces):
        k = lax.rem(peer(i), half)
        right[k, 0 : circum + 8, :] = piece[...]
        right[k, circum + 8 : rows, :] = piece[circum : circum + 8, :]

    def solve(rhs, below, k):
        rhs_hi, rhs_lo = split(rhs)
        below_hi, below_lo = split(below)
        left = jnp.concatenate(
            [
                jnp.concatenate([rhs_hi, below_hi], axis=1),
                jnp.concatenate([rhs_lo, below_lo], axis=1),
            ],
            axis=0,
        )
        product = lax.dot_general(
            left, weights[first + k], (((1,), (1,)), ((), ())), preferred_element_type=F32
        )
        high, low = product[:rows], product[rows:]
        cross = low[:, :block_rows] + high[:, block_rows:]
        return (high[:, :block_rows] + cross) + low[:, block_rows:]

    def advance(fields, k, sweep):
        rhs = right[k]
        if sweep > 0:
            around = pltpu.roll(fields[sweep - 1], 1, 0)
            around += pltpu.roll(fields[sweep - 1], rows - 1, 0)
            rhs = rhs + coupling * around
        return solve(rhs, fields[sweep], k)

    fields = list(fields)
    for wave in range(half + ITERS - 1):
        active = [j for j in range(ITERS) if 0 <= wave - j < half]
        news = [advance(fields, wave - j, j) for j in active]
        for j, new in zip(active, news, strict=True):
            fields[j] = new
        if wave >= ITERS - 1:
            solved[wave - ITERS + 1] = fields[-1][:circum]
    return fields


def stack_kernel(*refs):
    *pieces, _, out = refs
    for i, piece in enumerate(pieces):
        out[i] = piece[...]


def operators_kernel(mine, partner, weights):
    block_rows = mine.shape[2]
    for i in range(weights.shape[0]):
        k = peer(i)
        source = (mine, partner)[i % 2]
        for matrix in range(2):
            part = slice(matrix * block_rows, (matrix + 1) * block_rows)
            hi, lo = split(source[i // 2, part, :])
            weights[k, 0:block_rows, part] = hi
            weights[k, block_rows : 2 * block_rows, part] = lo


def lower_kernel(half, near, *refs):
    *rest, weights, state, solved, right = refs
    pieces = [rest[i] for i in near]
    upper = lax.axis_index("span") // half
    zero = jnp.zeros(state.shape[1:], F32)

    @pl.when(upper == 0)
    def _():
        for sweep, field in enumerate(
            solve_half(pieces, weights, 0, [zero] * ITERS, right, solved)
        ):
            state[sweep] = field

    @pl.when(upper != 0)
    def _():
        for sweep in range(ITERS):
            state[sweep] = zero


def far_kernel(half, *refs):
    pieces, (weights, state) = refs[:half], refs[half : half + 2]
    outs = refs[half + 2 : 2 * half + 2]
    after, right, solved = refs[2 * half + 2 :]
    upper = lax.axis_index("span") // half
    fields = solve_half(
        pieces, weights, (1 - upper) * half, [state[i] for i in range(ITERS)], right, solved
    )
    for i, out in enumerate(outs):
        out[...] = solved[lax.rem(peer(i), half)]
    for sweep, field in enumerate(fields):
        after[sweep] = field


def upper_kernel(half, *refs):
    pieces, (weights, state, done) = refs[:half], refs[half : half + 3]
    outs = refs[half + 3 : 2 * half + 3]
    right, solved = refs[2 * half + 3 :]
    upper = lax.axis_index("span") // half

    @pl.when(upper == 0)
    def _():
        for i, out in enumerate(outs):
            out[...] = done[lax.rem(peer(i), half)]

    @pl.when(upper != 0)
    def _():
        solve_half(pieces, weights, half, [state[i] for i in range(ITERS)], right, solved)
        for i, out in enumerate(outs):
            out[...] = solved[lax.rem(peer(i), half)]


def place_kernel(order, *refs):
    *pieces, out, sems = refs
    copies = [
        pltpu.make_async_copy(piece, out.at[peer(i)], sems.at[i])
        for i, piece in zip(order, pieces, strict=True)
    ]
    for copy in copies:
        copy.start()
    for copy in copies:
        copy.wait()


def exchange(array, axis, bits):
    count = lax.axis_size(axis)
    return lax.ppermute(array, axis, [(i, i ^ bits) for i in range(count)])


def by_harmonics(adj_source, face_flux, face_owner, face_cell, block_inverse, carry_gain):
    harm_rows, circum, block_rows = adj_source.shape
    count = lax.axis_size("span")
    half = count // 2
    near, far, diag, operators = pack(
        adj_source, face_flux, face_owner, face_cell, block_inverse, carry_gain
    )
    messages = [
        exchange(near, "blade", 1),
        exchange(far, "blade", 2),
        exchange(diag, "blade", 3),
    ]
    operators = [operators] + [exchange(operators, "span", bits) for bits in range(2, count, 2)]
    first, second = (4, 5, 6, 3), (2, 7, 1, 0)
    start = own_faces(first, far, circum)
    *pieces, token = right_pieces(
        first, False, adj_source, start, messages, [], "right_first"
    )
    right_side = dict(zip(first, pieces, strict=True))
    mine = call(
        stack_kernel,
        (((half, *operators[0].shape), F32),),
        [VMEM] * half + [ANY],
        [],
        0,
        "stack",
    )(*operators, token)[0]
    partner = exchange(mine, "span", 1)
    weights = call(
        operators_kernel,
        (((count, 2 * block_rows, 2 * block_rows), BF16),),
        [VMEM] * 2,
        [],
        0,
        "operators",
    )(mine, partner)[0]
    *pieces, _ = right_pieces(
        second, True, adj_source, far, messages, [token, weights], "right_second"
    )
    right_side |= dict(zip(second, pieces, strict=True))
    far_peers, near_peers = range(half, count), range(half)
    far_right = [exchange(right_side[i], "span", i) for i in far_peers]
    near_right = [right_side[0]] + [exchange(right_side[i], "span", i) for i in near_peers[1:]]

    rows = circum + 16
    right = pltpu.VMEM((half, rows, block_rows), F32)
    solved = pltpu.VMEM((half, circum, block_rows), F32)
    state_shape = ((ITERS, rows, block_rows), F32)
    piece = ((circum, block_rows), F32)
    state, done = call(
        functools.partial(lower_kernel, half, (6, 5, 3, 2)),
        (state_shape, ((half, circum, block_rows), F32)),
        [ANY, ANY, VMEM, VMEM, ANY, VMEM, VMEM, VMEM],
        [right],
        1_000_000_000,
        "sweeps_lower",
    )(far_right[0], far_right[1], near_right[3], near_right[2], far_right[2], near_right[1], near_right[0], weights)
    *far_solved, state = call(
        functools.partial(far_kernel, half),
        (piece,) * half + (state_shape,),
        [VMEM] * (half + 2),
        [right, solved],
        1_000_000_000,
        "sweeps_far",
    )(*far_right, weights, state)
    far_solved = [exchange(p, "span", i) for p, i in zip(far_solved, far_peers, strict=True)]
    near_solved = call(
        functools.partial(upper_kernel, half),
        (piece,) * half,
        [VMEM] * (half + 3),
        [right, solved],
        1_000_000_000,
        "sweeps_upper",
    )(*near_right, weights, state, done)
    near_solved = [p if i == 0 else exchange(p, "span", i) for i, p in enumerate(near_solved)]
    order = (4, 5, 6, 3, 2, 7, 1, 0)
    pieces = [*near_solved, *far_solved]
    return call(
        functools.partial(place_kernel, order),
        (((count, circum, block_rows), F32),),
        [ANY] * count,
        [pltpu.SemaphoreType.DMA((count,))],
        0,
        "place",
        out_specs=(ANY,),
    )(*[pieces[i] for i in order])[0]


def extended(block, sides, width):
    for axis, dim in sides:
        count = lax.axis_size(axis)
        forward = [(i, i + 1) for i in range(count - 1)]
        forward.append((count - 1, 0))
        backward = [(target, source) for source, target in forward]
        low = lax.ppermute(
            lax.slice_in_dim(block, block.shape[dim] - width, None, axis=dim), axis, forward
        )
        high = lax.ppermute(lax.slice_in_dim(block, 0, width, axis=dim), axis, backward)
        block = jnp.concatenate([low, block, high], axis=dim)
    return block


def pencil_solve(pencil, blocks, gains):
    harm_rows, columns, radial = pencil.shape
    nblocks, block_rows, _ = blocks.shape
    lines_all = pencil.reshape(harm_rows * columns, nblocks, block_rows)
    product = jnp.einsum("ckj,kij->kci", lines_all, blocks, precision=highest)

    def advance(running, element):
        local_part, gain = element
        updated = local_part + lax.dot_general(
            running,
            gain,
            (((1,), (1,)), ((), ())),
            precision=highest,
            preferred_element_type=jnp.float32,
        )
        return (updated, updated)

    initial = jnp.zeros((harm_rows * columns, block_rows), jnp.float32)
    _, solved = lax.scan(advance, initial, (product, gains))
    return jnp.transpose(solved, (1, 0, 2)).reshape(harm_rows, columns, radial)


def row_rhs(right_side, field):
    widened = extended(field, (("blade", 1),), 1)
    return right_side + coupling * (widened[:, :-2, :] + widened[:, 2:, :])


def by_lines(adj_source, face_flux, face_owner, face_cell, block_inverse, carry_gain):
    harm_rows, circum, block_rows = adj_source.shape
    blades = lax.axis_size("blade")
    faces_dev = face_owner.shape[0]
    capacity = faces_dev // 2
    onehot = (face_owner[:, None] == jnp.arange(blades, dtype=jnp.int32)[None, :]).astype(jnp.int32)
    rank_in = jnp.sum((jnp.cumsum(onehot, axis=0) - 1) * onehot, axis=1)
    slot_ids = face_owner * capacity + rank_in
    send_flux = (
        jnp.zeros((harm_rows, blades * capacity), jnp.float32)
        .at[:, slot_ids]
        .set(face_flux)
        .reshape(harm_rows, blades, capacity)
    )
    send_cell = (
        jnp.zeros((blades * capacity,), jnp.int32)
        .at[slot_ids]
        .set(face_cell)
        .reshape(1, blades, capacity)
    )
    fluxes, cell_ids = (
        lax.all_to_all(send_flux, "blade", split_axis=1, concat_axis=1, tiled=True),
        lax.all_to_all(send_cell, "blade", split_axis=1, concat_axis=1, tiled=True),
    )
    fluxes = fluxes.reshape(harm_rows, blades * capacity)
    cell_ids = cell_ids.reshape(blades * capacity)
    wall_flux = jnp.zeros((harm_rows, circum * block_rows), jnp.float32).at[:, cell_ids].add(fluxes)
    right_side = adj_source + wall_flux.reshape(harm_rows, circum, block_rows)
    inverses, couplings = (
        lax.all_gather(block_inverse, "span", axis=0, tiled=True),
        lax.all_gather(carry_gain, "span", axis=0, tiled=True),
    )
    blocks = inverses.reshape(-1, block_rows, block_rows)
    gains = couplings.reshape(-1, block_rows, block_rows)

    def transposed(rhs_rows):
        pencil = lax.all_to_all(rhs_rows, "span", split_axis=1, concat_axis=2, tiled=True)
        return lax.all_to_all(
            pencil_solve(pencil, blocks, gains), "span", split_axis=2, concat_axis=1, tiled=True
        )

    field = transposed(right_side)
    for sweep_index in range(1, ITERS):
        field = transposed(row_rhs(right_side, field))
    return field


def body(adj_source, *others):
    harm_rows, circum, block_rows = adj_source.shape
    if lax.axis_size("span") == harm_rows == 8 and lax.axis_size("blade") == 4:
        return by_harmonics(adj_source, *others)
    return by_lines(adj_source, *others)


def solution(mesh):
    in_specs = (
        P(None, "blade", "span"),
        P(None, ("blade", "span")),
        P(("blade", "span")),
        P(("blade", "span")),
        P("span", None),
        P("span", None),
    )
    out_specs = P(None, "blade", "span")
    return jax.shard_map(body, mesh=mesh, in_specs=in_specs, out_specs=out_specs, check_vma=False)
```

```python
import functools

import jax
import jax.numpy as jnp
from jax import lax
from jax.experimental import pallas as pl
from jax.experimental.pallas import tpu as pltpu
from jax.sharding import PartitionSpec as P

ITERS = 3
HALO = ITERS - 1

coupling = 0.05
highest = lax.Precision.HIGHEST
VMEM = pl.BlockSpec(memory_space=pltpu.VMEM)
ANY = pl.BlockSpec(memory_space=pl.ANY)
HBM = pl.BlockSpec(memory_space=pltpu.HBM)
F32 = jnp.float32
BF16 = jnp.bfloat16


def call(kernel, outs, ins, scratch, flops, name, out_specs=None, vmem=24):
    shapes = tuple(jax.ShapeDtypeStruct(shape, dtype) for shape, dtype in outs)
    return pl.pallas_call(
        kernel,
        out_shape=shapes,
        in_specs=ins,
        out_specs=out_specs or (VMEM,) * len(outs),
        scratch_shapes=scratch,
        compiler_params=pltpu.CompilerParams(vmem_limit_bytes=vmem * 1024 * 1024),
        cost_estimate=pl.CostEstimate(flops=flops, bytes_accessed=1 << 20, transcendentals=0),
        name=name,
    )


def split(x):
    hi = x.astype(BF16)
    return hi, (x - hi.astype(F32)).astype(BF16)


def peer(i):
    return lax.bitwise_xor(lax.axis_index("span"), i)


def pack_kernel(flux, owner, cell, first, last, near, far, diag):
    groups = owner.shape[0]
    odd = lax.rem(lax.axis_index("blade"), 2)
    for message in (near, far, diag):
        for group in range(groups):
            message[group] = flux[:, group * 128 : (group + 1) * 128]
        message[groups] = owner[...].astype(F32)
        message[groups + 1] = cell[...].astype(F32)
    for row in range(HALO):
        low = first[:, row, :]
        high = last[:, 8 - HALO + row, :]
        near[groups + 2 + row] = jnp.where(odd == 0, high, low)
        diag[groups + 2 + row] = jnp.where(odd == 0, low, high)


def pack(adj_source, face_flux, face_owner, face_cell):
    groups = face_owner.shape[0] // 128
    circum = adj_source.shape[1]
    with_halo = ((groups + 2 + HALO, 8, 128), F32)
    faces = ((groups + 2, 8, 128), F32)
    return call(
        pack_kernel,
        (with_halo, faces, with_halo),
        [VMEM] * 5,
        [],
        0,
        "pack",
    )(
        face_flux,
        face_owner.reshape(groups, 128),
        face_cell.reshape(groups, 128),
        adj_source[:, :8],
        adj_source[:, circum - 8 :],
    )


def face_product(message, hot_rows, weights, harmonics, circum, block_rows):
    blades = lax.axis_size("blade")
    blade = lax.axis_index("blade")
    total = circum * blades
    groups = weights.shape[1] // 256
    rows = hot_rows.shape[0]
    row = lax.broadcasted_iota(jnp.int32, (rows, 128), 0)
    label = jnp.where(
        row < circum + HALO,
        row,
        jnp.where(
            (row >= circum + 8 - HALO) & (row < circum + 8), row - (circum + 8) + total, -1
        ),
    )
    radial = lax.broadcasted_iota(jnp.int32, (block_rows, 128), 0)
    owner = message[groups].astype(jnp.int32)
    cell = message[groups + 1].astype(jnp.int32)
    place = (owner - blade) * circum + cell // block_rows
    place = jnp.where(place < 0, place + total, place)
    inner = cell % block_rows
    for group in range(groups):
        lanes = slice(group * 128, (group + 1) * 128)
        lanes_low = slice((groups + group) * 128, (groups + group + 1) * 128)
        hot = jnp.where(label == place[group : group + 1, :], 1.0, 0.0).astype(BF16)
        hot_rows[:, lanes] = hot
        hot_rows[:, lanes_low] = hot
        hit = jnp.where(radial == inner[group : group + 1, :], 1.0, 0.0).astype(BF16)
        hit = hit.reshape(block_rows // 16, 16, 128)
        for at, h in enumerate(harmonics):
            flux = jnp.broadcast_to(message[group, pl.ds(h, 1), :], (16, 128))
            flux_hi, flux_lo = split(flux)
            part = slice(at * block_rows, (at + 1) * block_rows)
            weights[part, lanes] = (hit * flux_hi[None]).reshape(block_rows, 128)
            weights[part, lanes_low] = (hit * flux_lo[None]).reshape(block_rows, 128)
    return lax.dot_general(
        hot_rows[...], weights[...], (((1,), (1,)), ((), ())), preferred_element_type=F32
    )


def face_sums_kernel(peers, *refs):
    *start, message, acc, hot_rows, weights = refs
    circum, block_rows = acc.shape[0] - 16, acc.shape[1] // len(peers)
    harmonics = [peer(i) for i in peers]
    sums = face_product(message, hot_rows, weights, harmonics, circum, block_rows)
    for before in start:
        sums += before[...]
    acc[...] = sums


def face_sums(peers, circum, block_rows, message, *start):
    faces = (message.shape[0] - 2) * 128
    rows, lanes = circum + 16, len(peers) * block_rows
    return call(
        functools.partial(face_sums_kernel, peers),
        (((rows, lanes), F32),),
        [VMEM] * (1 + len(start)),
        [pltpu.VMEM((rows, 2 * faces), BF16), pltpu.VMEM((lanes, 2 * faces), BF16)],
        600_000_000,
        "face_sums",
    )(*start, message)[0]


def right_kernel(peers, own, adj, start, diag, near, far, *rest):
    count = len(peers)
    *outs, hot_rows, weights, acc, source, sems = rest
    del outs[: len(outs) - count - 1]
    outs[count][...] = jnp.zeros_like(outs[count])
    _, circum, block_rows = adj.shape
    copies = [
        pltpu.make_async_copy(adj.at[peer(i)], source.at[at], sems.at[at])
        for at, i in enumerate(peers)
    ]
    for copy in copies:
        copy.start()
    groups = weights.shape[2] // 256
    odd = lax.rem(lax.axis_index("blade"), 2)
    harmonics = [peer(i) for i in peers]
    messages = (start, near, far, diag) if own else (diag, near)
    if not own:
        acc[...] = start[...]
    for step, message in enumerate(messages):
        product = face_product(
            message, hot_rows.at[step], weights.at[step], harmonics, circum, block_rows
        )
        if own and step == 0:
            acc[...] = product
        else:
            acc[...] += product
    gap = jnp.zeros((8 - 2 * HALO, 128), F32)
    for copy in copies:
        copy.wait()
    for at, (i, out) in enumerate(zip(peers, outs[:count], strict=True)):
        row = pl.ds(peer(i), 1)
        one = [near[groups + 2 + j, row, :] for j in range(HALO)]
        three = [diag[groups + 2 + j, row, :] for j in range(HALO)]
        above = [jnp.where(odd == 0, a, b) for a, b in zip(one, three, strict=True)]
        below = [jnp.where(odd == 0, b, a) for a, b in zip(one, three, strict=True)]
        part = slice(at * block_rows, (at + 1) * block_rows)
        out[0:circum, :] = source[at] + acc[0:circum, part]
        out[circum : circum + 8, :] = acc[circum : circum + 8, part] + jnp.concatenate(
            above + [gap] + below, axis=0
        )


def right_pieces(peers, own, adj_source, start, messages, after, name):
    _, circum, block_rows = adj_source.shape
    count = len(peers)
    faces = (min(m.shape[0] for m in messages) - 2) * 128
    rows = circum + 16
    sums = 4 if own else 2
    return call(
        functools.partial(right_kernel, peers, own),
        (((circum + 8, block_rows), F32),) * count + (((8, 128), F32),),
        [HBM] + [VMEM] * 4 + [ANY] * len(after),
        [
            pltpu.VMEM((sums, rows, 2 * faces), BF16),
            pltpu.VMEM((sums, count * block_rows, 2 * faces), BF16),
            pltpu.VMEM((rows, count * block_rows), F32),
            pltpu.VMEM((count, circum, block_rows), F32),
            pltpu.SemaphoreType.DMA((count,)),
        ],
        600_000_000 * sums,
        name,
    )(adj_source, start, *messages, *after)


def solve_half(pieces, weights, first, fields, right, solved):
    half = len(pieces)
    rows, block_rows = right.shape[1:]
    circum = rows - 16
    for i, piece in enumerate(pieces):
        k = lax.rem(peer(i), half)
        right[k, 0 : circum + 8, :] = piece[...]
        right[k, circum + 8 : rows, :] = piece[circum : circum + 8, :]

    def solve(rhs, below, k):
        rhs_hi, rhs_lo = split(rhs)
        below_hi, below_lo = split(below)
        left = jnp.concatenate(
            [
                jnp.concatenate([rhs_hi, below_hi], axis=1),
                jnp.concatenate([rhs_lo, below_lo], axis=1),
            ],
            axis=0,
        )
        product = lax.dot_general(
            left, weights[first + k], (((1,), (1,)), ((), ())), preferred_element_type=F32
        )
        high, low = product[:rows], product[rows:]
        cross = low[:, :block_rows] + high[:, block_rows:]
        return (high[:, :block_rows] + cross) + low[:, block_rows:]

    def advance(fields, k, sweep):
        rhs = right[k]
        if sweep > 0:
            around = pltpu.roll(fields[sweep - 1], 1, 0)
            around += pltpu.roll(fields[sweep - 1], rows - 1, 0)
            rhs = rhs + coupling * around
        return solve(rhs, fields[sweep], k)

    fields = list(fields)
    for wave in range(half + ITERS - 1):
        active = [j for j in range(ITERS) if 0 <= wave - j < half]
        news = [advance(fields, wave - j, j) for j in active]
        for j, new in zip(active, news, strict=True):
            fields[j] = new
        if wave >= ITERS - 1:
            solved[wave - ITERS + 1] = fields[-1][:circum]
    return fields


def stack_kernel(*refs):
    *pieces, out = refs
    at = 0
    for piece in pieces:
        if piece.shape[0] > 8:
            out[at : at + piece.shape[0], :] = piece[...]
            at += piece.shape[0]


def stack(*pieces):
    rows = sum(piece.shape[0] for piece in pieces if piece.shape[0] > 8)
    return call(
        stack_kernel,
        (((rows, pieces[0].shape[1]), F32),),
        [VMEM] * len(pieces),
        [],
        0,
        "stack",
    )(*pieces)[0]


def operators_kernel(chip, across, partner, weights):
    block_rows = chip.shape[1]
    first = 2 + 2 * lax.rem(lax.axis_index("span"), 2)
    second = lax.bitwise_xor(first, 6)
    places = (
        (chip, (0, 1)),
        (across, (first, first + 1, 6)),
        (partner, (second + 1, second, 7)),
    )
    for source, bits in places:
        for at, i in enumerate(bits):
            k = peer(i)
            for matrix in range(2):
                low = (2 * at + matrix) * block_rows
                part = slice(matrix * block_rows, (matrix + 1) * block_rows)
                hi, lo = split(source[low : low + block_rows, :])
                weights[k, 0:block_rows, part] = hi
                weights[k, block_rows : 2 * block_rows, part] = lo


def lower_kernel(half, near, *refs):
    *rest, weights, state, solved, right = refs
    pieces = [rest[i] for i in near]
    upper = lax.axis_index("span") // half
    zero = jnp.zeros(state.shape[1:], F32)

    @pl.when(upper == 0)
    def _():
        for sweep, field in enumerate(
            solve_half(pieces, weights, 0, [zero] * ITERS, right, solved)
        ):
            state[sweep] = field

    @pl.when(upper != 0)
    def _():
        for sweep in range(ITERS):
            state[sweep] = zero


def far_kernel(half, *refs):
    pieces, (weights, state) = refs[:half], refs[half : half + 2]
    outs = refs[half + 2 : 2 * half + 2]
    after, right, solved = refs[2 * half + 2 :]
    upper = lax.axis_index("span") // half
    fields = solve_half(
        pieces, weights, (1 - upper) * half, [state[i] for i in range(ITERS)], right, solved
    )
    for i, out in enumerate(outs):
        out[...] = solved[lax.rem(peer(i), half)]
    for sweep, field in enumerate(fields):
        after[sweep] = field


def upper_kernel(half, *refs):
    pieces, (weights, state, done) = refs[:half], refs[half : half + 3]
    outs = refs[half + 3 : 2 * half + 3]
    right, solved = refs[2 * half + 3 :]
    upper = lax.axis_index("span") // half

    @pl.when(upper == 0)
    def _():
        for i, out in enumerate(outs):
            out[...] = done[lax.rem(peer(i), half)]

    @pl.when(upper != 0)
    def _():
        solve_half(pieces, weights, half, [state[i] for i in range(ITERS)], right, solved)
        for i, out in enumerate(outs):
            out[...] = solved[lax.rem(peer(i), half)]


def place_kernel(order, *refs):
    *pieces, out, sems = refs
    copies = [
        pltpu.make_async_copy(piece, out.at[peer(i)], sems.at[i])
        for i, piece in zip(order, pieces, strict=True)
    ]
    for copy in copies:
        copy.start()
    for copy in copies:
        copy.wait()


def exchange(array, axis, bits):
    count = lax.axis_size(axis)
    return lax.ppermute(array, axis, [(i, i ^ bits) for i in range(count)])


def by_harmonics(adj_source, face_flux, face_owner, face_cell, block_inverse, carry_gain):
    harm_rows, circum, block_rows = adj_source.shape
    count = lax.axis_size("span")
    half = count // 2
    operators = jnp.concatenate([block_inverse, carry_gain], axis=0)
    near, far, diag = pack(adj_source, face_flux, face_owner, face_cell)
    messages = [
        exchange(diag, "blade", 3),
        exchange(near, "blade", 1),
        exchange(far, "blade", 2),
    ]
    chip = stack(operators, exchange(operators, "span", 1))
    apart = lax.ppermute(chip, "span", [(i, i ^ (2 + 2 * (i % 2))) for i in range(count)])
    farthest = exchange(operators, "span", 6)
    first, second = (4, 5, 6, 3), (2, 7, 1, 0)
    start = face_sums(first, circum, block_rows, far)
    start = face_sums(first, circum, block_rows, messages[2], start)
    *pieces, token = right_pieces(
        first, False, adj_source, start, messages, [], "right_first"
    )
    right_side = dict(zip(first, pieces, strict=True))
    across = stack(apart, farthest, token)
    partner = exchange(across, "span", 1)
    weights = call(
        operators_kernel,
        (((count, 2 * block_rows, 2 * block_rows), BF16),),
        [VMEM] * 3,
        [],
        0,
        "operators",
    )(chip, across, partner)[0]
    *pieces, _ = right_pieces(
        second, True, adj_source, far, messages, [token, weights], "right_second"
    )
    right_side |= dict(zip(second, pieces, strict=True))
    far_peers, near_peers = range(half, count), range(half)
    far_right = [exchange(right_side[i], "span", i) for i in far_peers]
    near_right = [right_side[0]] + [exchange(right_side[i], "span", i) for i in near_peers[1:]]

    rows = circum + 16
    right = pltpu.VMEM((half, rows, block_rows), F32)
    solved = pltpu.VMEM((half, circum, block_rows), F32)
    state_shape = ((ITERS, rows, block_rows), F32)
    piece = ((circum, block_rows), F32)
    state, done = call(
        functools.partial(lower_kernel, half, (6, 5, 3, 2)),
        (state_shape, ((half, circum, block_rows), F32)),
        [ANY, ANY, VMEM, VMEM, ANY, VMEM, VMEM, VMEM],
        [right],
        1_000_000_000,
        "sweeps_lower",
    )(far_right[0], far_right[1], near_right[3], near_right[2], far_right[2], near_right[1], near_right[0], weights)
    *far_solved, state = call(
        functools.partial(far_kernel, half),
        (piece,) * half + (state_shape,),
        [VMEM] * (half + 2),
        [right, solved],
        1_000_000_000,
        "sweeps_far",
    )(*far_right, weights, state)
    far_solved = [exchange(p, "span", i) for p, i in zip(far_solved, far_peers, strict=True)]
    near_solved = call(
        functools.partial(upper_kernel, half),
        (piece,) * half,
        [VMEM] * (half + 3),
        [right, solved],
        1_000_000_000,
        "sweeps_upper",
    )(*near_right, weights, state, done)
    near_solved = [p if i == 0 else exchange(p, "span", i) for i, p in enumerate(near_solved)]
    order = (4, 5, 6, 3, 2, 7, 1, 0)
    pieces = [*near_solved, *far_solved]
    return call(
        functools.partial(place_kernel, order),
        (((count, circum, block_rows), F32),),
        [ANY] * count,
        [pltpu.SemaphoreType.DMA((count,))],
        0,
        "place",
        out_specs=(ANY,),
    )(*[pieces[i] for i in order])[0]


def extended(block, sides, width):
    for axis, dim in sides:
        count = lax.axis_size(axis)
        forward = [(i, i + 1) for i in range(count - 1)]
        forward.append((count - 1, 0))
        backward = [(target, source) for source, target in forward]
        low = lax.ppermute(
            lax.slice_in_dim(block, block.shape[dim] - width, None, axis=dim), axis, forward
        )
        high = lax.ppermute(lax.slice_in_dim(block, 0, width, axis=dim), axis, backward)
        block = jnp.concatenate([low, block, high], axis=dim)
    return block


def pencil_solve(pencil, blocks, gains):
    harm_rows, columns, radial = pencil.shape
    nblocks, block_rows, _ = blocks.shape
    lines_all = pencil.reshape(harm_rows * columns, nblocks, block_rows)
    product = jnp.einsum("ckj,kij->kci", lines_all, blocks, precision=highest)

    def advance(running, element):
        local_part, gain = element
        updated = local_part + lax.dot_general(
            running,
            gain,
            (((1,), (1,)), ((), ())),
            precision=highest,
            preferred_element_type=jnp.float32,
        )
        return (updated, updated)

    initial = jnp.zeros((harm_rows * columns, block_rows), jnp.float32)
    _, solved = lax.scan(advance, initial, (product, gains))
    return jnp.transpose(solved, (1, 0, 2)).reshape(harm_rows, columns, radial)


def row_rhs(right_side, field):
    widened = extended(field, (("blade", 1),), 1)
    return right_side + coupling * (widened[:, :-2, :] + widened[:, 2:, :])


def by_lines(adj_source, face_flux, face_owner, face_cell, block_inverse, carry_gain):
    harm_rows, circum, block_rows = adj_source.shape
    blades = lax.axis_size("blade")
    faces_dev = face_owner.shape[0]
    capacity = faces_dev // 2
    onehot = (face_owner[:, None] == jnp.arange(blades, dtype=jnp.int32)[None, :]).astype(jnp.int32)
    rank_in = jnp.sum((jnp.cumsum(onehot, axis=0) - 1) * onehot, axis=1)
    slot_ids = face_owner * capacity + rank_in
    send_flux = (
        jnp.zeros((harm_rows, blades * capacity), jnp.float32)
        .at[:, slot_ids]
        .set(face_flux)
        .reshape(harm_rows, blades, capacity)
    )
    send_cell = (
        jnp.zeros((blades * capacity,), jnp.int32)
        .at[slot_ids]
        .set(face_cell)
        .reshape(1, blades, capacity)
    )
    fluxes, cell_ids = (
        lax.all_to_all(send_flux, "blade", split_axis=1, concat_axis=1, tiled=True),
        lax.all_to_all(send_cell, "blade", split_axis=1, concat_axis=1, tiled=True),
    )
    fluxes = fluxes.reshape(harm_rows, blades * capacity)
    cell_ids = cell_ids.reshape(blades * capacity)
    wall_flux = jnp.zeros((harm_rows, circum * block_rows), jnp.float32).at[:, cell_ids].add(fluxes)
    right_side = adj_source + wall_flux.reshape(harm_rows, circum, block_rows)
    inverses, couplings = (
        lax.all_gather(block_inverse, "span", axis=0, tiled=True),
        lax.all_gather(carry_gain, "span", axis=0, tiled=True),
    )
    blocks = inverses.reshape(-1, block_rows, block_rows)
    gains = couplings.reshape(-1, block_rows, block_rows)

    def transposed(rhs_rows):
        pencil = lax.all_to_all(rhs_rows, "span", split_axis=1, concat_axis=2, tiled=True)
        return lax.all_to_all(
            pencil_solve(pencil, blocks, gains), "span", split_axis=2, concat_axis=1, tiled=True
        )

    field = transposed(right_side)
    for sweep_index in range(1, ITERS):
        field = transposed(row_rhs(right_side, field))
    return field


def body(adj_source, *others):
    harm_rows, circum, block_rows = adj_source.shape
    if lax.axis_size("span") == harm_rows == 8 and lax.axis_size("blade") == 4:
        return by_harmonics(adj_source, *others)
    return by_lines(adj_source, *others)


def solution(mesh):
    in_specs = (
        P(None, "blade", "span"),
        P(None, ("blade", "span")),
        P(("blade", "span")),
        P(("blade", "span")),
        P("span", None),
        P("span", None),
    )
    out_specs = P(None, "blade", "span")
    return jax.shard_map(body, mesh=mesh, in_specs=in_specs, out_specs=out_specs, check_vma=False)
```

```python
import functools

import jax
import jax.numpy as jnp
from jax import lax
from jax.experimental import pallas as pl
from jax.experimental.pallas import tpu as pltpu
from jax.sharding import PartitionSpec as P

ITERS = 3
HALO = ITERS - 1

coupling = 0.05
highest = lax.Precision.HIGHEST
VMEM = pl.BlockSpec(memory_space=pltpu.VMEM)
ANY = pl.BlockSpec(memory_space=pl.ANY)
HBM = pl.BlockSpec(memory_space=pltpu.HBM)
F32 = jnp.float32
BF16 = jnp.bfloat16


def call(kernel, outs, ins, scratch, flops, name, out_specs=None, vmem=24):
    shapes = tuple(jax.ShapeDtypeStruct(shape, dtype) for shape, dtype in outs)
    return pl.pallas_call(
        kernel,
        out_shape=shapes,
        in_specs=ins,
        out_specs=out_specs or (VMEM,) * len(outs),
        scratch_shapes=scratch,
        compiler_params=pltpu.CompilerParams(vmem_limit_bytes=vmem * 1024 * 1024),
        cost_estimate=pl.CostEstimate(flops=flops, bytes_accessed=1 << 20, transcendentals=0),
        name=name,
    )


def split(x):
    hi = x.astype(BF16)
    return hi, (x - hi.astype(F32)).astype(BF16)


def peer(i):
    return lax.bitwise_xor(lax.axis_index("span"), i)


def pack_kernel(flux, owner, cell, first, last, near, far, diag):
    groups = owner.shape[0]
    odd = lax.rem(lax.axis_index("blade"), 2)
    for message in (near, far, diag):
        for group in range(groups):
            message[group] = flux[:, group * 128 : (group + 1) * 128]
        message[groups] = owner[...].astype(F32)
        message[groups + 1] = cell[...].astype(F32)
    for row in range(HALO):
        low = first[:, row, :]
        high = last[:, 8 - HALO + row, :]
        near[groups + 2 + row] = jnp.where(odd == 0, high, low)
        diag[groups + 2 + row] = jnp.where(odd == 0, low, high)


def pack(adj_source, face_flux, face_owner, face_cell):
    groups = face_owner.shape[0] // 128
    circum = adj_source.shape[1]
    with_halo = ((groups + 2 + HALO, 8, 128), F32)
    faces = ((groups + 2, 8, 128), F32)
    return call(
        pack_kernel,
        (with_halo, faces, with_halo),
        [VMEM] * 5,
        [],
        0,
        "pack",
    )(
        face_flux,
        face_owner.reshape(groups, 128),
        face_cell.reshape(groups, 128),
        adj_source[:, :8],
        adj_source[:, circum - 8 :],
    )


def face_product(message, hot_rows, weights, harmonics, circum, block_rows):
    blades = lax.axis_size("blade")
    blade = lax.axis_index("blade")
    total = circum * blades
    faces = hot_rows.shape[1]
    groups = faces // 128
    rows = hot_rows.shape[0]
    row = lax.broadcasted_iota(jnp.int32, (rows, 128), 0)
    label = jnp.where(
        row < circum + HALO,
        row,
        jnp.where(
            (row >= circum + 8 - HALO) & (row < circum + 8), row - (circum + 8) + total, -1
        ),
    )
    radial = lax.broadcasted_iota(jnp.int32, (block_rows, 128), 0).astype(F32).astype(BF16)
    zero = jnp.zeros((), BF16)
    owner = message[groups].astype(jnp.int32)
    cell = message[groups + 1].astype(jnp.int32)
    place = (owner - blade) * circum + cell // block_rows
    place = jnp.where(place < 0, place + total, place)
    inner = cell % block_rows
    def wide(row):
        return jnp.broadcast_to(row[None], (block_rows // 16, 16, 128)).reshape(block_rows, 128)

    for group in range(groups):
        lanes = slice(group * 128, (group + 1) * 128)
        lanes_low = slice((groups + group) * 128, (groups + group + 1) * 128)
        hot = jnp.where(label == place[group : group + 1, :], 1.0, 0.0).astype(BF16)
        hot_rows[:, lanes] = hot
        here = jnp.broadcast_to(inner[group : group + 1, :], (block_rows, 128)).astype(F32)
        hit = radial == here.astype(BF16)
        for at, h in enumerate(harmonics):
            flux = jnp.broadcast_to(message[group, pl.ds(h, 1), :], (16, 128))
            flux_hi, flux_lo = split(flux)
            part = slice(at * block_rows, (at + 1) * block_rows)
            weights[part, lanes] = jnp.where(hit, wide(flux_hi), zero)
            weights[part, lanes_low] = jnp.where(hit, wide(flux_lo), zero)
    high, low = (
        lax.dot_general(
            hot_rows[...],
            weights[:, part],
            (((1,), (1,)), ((), ())),
            preferred_element_type=F32,
        )
        for part in (slice(0, faces), slice(faces, 2 * faces))
    )
    return high + low


def face_sums_kernel(peers, *refs):
    *start, message, acc, hot_rows, weights = refs
    circum, block_rows = acc.shape[0] - 16, acc.shape[1] // len(peers)
    harmonics = [peer(i) for i in peers]
    sums = face_product(message, hot_rows, weights, harmonics, circum, block_rows)
    for before in start:
        sums += before[...]
    acc[...] = sums


def face_sums(peers, circum, block_rows, message, *start):
    faces = (message.shape[0] - 2) * 128
    rows, lanes = circum + 16, len(peers) * block_rows
    return call(
        functools.partial(face_sums_kernel, peers),
        (((rows, lanes), F32),),
        [VMEM] * (1 + len(start)),
        [pltpu.VMEM((rows, faces), BF16), pltpu.VMEM((lanes, 2 * faces), BF16)],
        600_000_000,
        "face_sums",
    )(*start, message)[0]


def right_kernel(peers, own, adj, start, diag, near, far, *rest):
    count = len(peers)
    *outs, hot_rows, weights, acc, source, sems = rest
    del outs[: len(outs) - count - 1]
    outs[count][...] = jnp.zeros_like(outs[count])
    _, circum, block_rows = adj.shape
    copies = [
        pltpu.make_async_copy(adj.at[peer(i)], source.at[at], sems.at[at])
        for at, i in enumerate(peers)
    ]
    for copy in copies:
        copy.start()
    groups = hot_rows.shape[2] // 128
    odd = lax.rem(lax.axis_index("blade"), 2)
    harmonics = [peer(i) for i in peers]
    messages = (start, near, far, diag) if own else (diag, near)
    if not own:
        acc[...] = start[...]
    for step, message in enumerate(messages):
        product = face_product(
            message, hot_rows.at[step], weights.at[step], harmonics, circum, block_rows
        )
        if own and step == 0:
            acc[...] = product
        else:
            acc[...] += product
    gap = jnp.zeros((8 - 2 * HALO, 128), F32)
    for copy in copies:
        copy.wait()
    for at, (i, out) in enumerate(zip(peers, outs[:count], strict=True)):
        row = pl.ds(peer(i), 1)
        one = [near[groups + 2 + j, row, :] for j in range(HALO)]
        three = [diag[groups + 2 + j, row, :] for j in range(HALO)]
        above = [jnp.where(odd == 0, a, b) for a, b in zip(one, three, strict=True)]
        below = [jnp.where(odd == 0, b, a) for a, b in zip(one, three, strict=True)]
        part = slice(at * block_rows, (at + 1) * block_rows)
        out[0:circum, :] = source[at] + acc[0:circum, part]
        out[circum : circum + 8, :] = acc[circum : circum + 8, part] + jnp.concatenate(
            above + [gap] + below, axis=0
        )


def right_pieces(peers, own, adj_source, start, messages, after, name):
    _, circum, block_rows = adj_source.shape
    count = len(peers)
    faces = (min(m.shape[0] for m in messages) - 2) * 128
    rows = circum + 16
    sums = 4 if own else 2
    return call(
        functools.partial(right_kernel, peers, own),
        (((circum + 8, block_rows), F32),) * count + (((8, 128), F32),),
        [HBM] + [VMEM] * 4 + [ANY] * len(after),
        [
            pltpu.VMEM((sums, rows, faces), BF16),
            pltpu.VMEM((sums, count * block_rows, 2 * faces), BF16),
            pltpu.VMEM((rows, count * block_rows), F32),
            pltpu.VMEM((count, circum, block_rows), F32),
            pltpu.SemaphoreType.DMA((count,)),
        ],
        600_000_000 * sums,
        name,
    )(adj_source, start, *messages, *after)


def solve_half(pieces, weights, first, fields, right, solved):
    half = len(pieces)
    rows, block_rows = right.shape[1:]
    circum = rows - 16
    for i, piece in enumerate(pieces):
        k = lax.rem(peer(i), half)
        right[k, 0 : circum + 8, :] = piece[...]
        right[k, circum + 8 : rows, :] = piece[circum : circum + 8, :]

    def solve(rhs, below, k):
        rhs_hi, rhs_lo = split(rhs)
        below_hi, below_lo = split(below)
        contract = (((1,), (1,)), ((), ()))
        high = lax.dot_general(
            jnp.concatenate([rhs_hi, below_hi], axis=1),
            weights[first + k],
            contract,
            preferred_element_type=F32,
        )
        low = lax.dot_general(
            jnp.concatenate([rhs_lo, below_lo], axis=1),
            weights[first + k, :block_rows],
            contract,
            preferred_element_type=F32,
        )
        return high[:, :block_rows] + (low + high[:, block_rows:])

    def advance(fields, k, sweep):
        rhs = right[k]
        if sweep > 0:
            around = pltpu.roll(fields[sweep - 1], 1, 0)
            around += pltpu.roll(fields[sweep - 1], rows - 1, 0)
            rhs = rhs + coupling * around
        return solve(rhs, fields[sweep], k)

    fields = list(fields)
    for wave in range(half + ITERS - 1):
        active = [j for j in range(ITERS) if 0 <= wave - j < half]
        news = [advance(fields, wave - j, j) for j in active]
        for j, new in zip(active, news, strict=True):
            fields[j] = new
        if wave >= ITERS - 1:
            solved[wave - ITERS + 1] = fields[-1][:circum]
    return fields


def stack_kernel(*refs):
    *pieces, out = refs
    at = 0
    for piece in pieces:
        if piece.shape[0] > 8:
            out[at : at + piece.shape[0], :] = piece[...]
            at += piece.shape[0]


def stack(*pieces):
    rows = sum(piece.shape[0] for piece in pieces if piece.shape[0] > 8)
    return call(
        stack_kernel,
        (((rows, pieces[0].shape[1]), F32),),
        [VMEM] * len(pieces),
        [],
        0,
        "stack",
    )(*pieces)[0]


def operators_kernel(chip, across, partner, weights):
    block_rows = chip.shape[1]
    first = 2 + 2 * lax.rem(lax.axis_index("span"), 2)
    second = lax.bitwise_xor(first, 6)
    places = (
        (chip, (0, 1)),
        (across, (first, first + 1, 6)),
        (partner, (second + 1, second, 7)),
    )
    for source, bits in places:
        for at, i in enumerate(bits):
            k = peer(i)
            for matrix in range(2):
                low = (2 * at + matrix) * block_rows
                part = slice(matrix * block_rows, (matrix + 1) * block_rows)
                hi, lo = split(source[low : low + block_rows, :])
                weights[k, 0:block_rows, part] = hi
                weights[k, block_rows : 2 * block_rows, part] = lo


def lower_kernel(half, near, *refs):
    *rest, weights, state, solved, right = refs
    pieces = [rest[i] for i in near]
    upper = lax.axis_index("span") // half
    zero = jnp.zeros(state.shape[1:], F32)

    @pl.when(upper == 0)
    def _():
        for sweep, field in enumerate(
            solve_half(pieces, weights, 0, [zero] * ITERS, right, solved)
        ):
            state[sweep] = field

    @pl.when(upper != 0)
    def _():
        for sweep in range(ITERS):
            state[sweep] = zero


def far_kernel(half, *refs):
    pieces, (weights, state) = refs[:half], refs[half : half + 2]
    outs = refs[half + 2 : 2 * half + 2]
    after, right, solved = refs[2 * half + 2 :]
    upper = lax.axis_index("span") // half
    fields = solve_half(
        pieces, weights, (1 - upper) * half, [state[i] for i in range(ITERS)], right, solved
    )
    for i, out in enumerate(outs):
        out[...] = solved[lax.rem(peer(i), half)]
    for sweep, field in enumerate(fields):
        after[sweep] = field


def upper_kernel(half, *refs):
    pieces, (weights, state, done) = refs[:half], refs[half : half + 3]
    outs = refs[half + 3 : 2 * half + 3]
    right, solved = refs[2 * half + 3 :]
    upper = lax.axis_index("span") // half

    @pl.when(upper == 0)
    def _():
        for i, out in enumerate(outs):
            out[...] = done[lax.rem(peer(i), half)]

    @pl.when(upper != 0)
    def _():
        solve_half(pieces, weights, half, [state[i] for i in range(ITERS)], right, solved)
        for i, out in enumerate(outs):
            out[...] = solved[lax.rem(peer(i), half)]


def place_kernel(order, *refs):
    *pieces, out, sems = refs
    copies = [
        pltpu.make_async_copy(piece, out.at[peer(i)], sems.at[i])
        for i, piece in zip(order, pieces, strict=True)
    ]
    for copy in copies:
        copy.start()
    for copy in copies:
        copy.wait()


def exchange(array, axis, bits):
    count = lax.axis_size(axis)
    return lax.ppermute(array, axis, [(i, i ^ bits) for i in range(count)])


def by_harmonics(adj_source, face_flux, face_owner, face_cell, block_inverse, carry_gain):
    harm_rows, circum, block_rows = adj_source.shape
    count = lax.axis_size("span")
    half = count // 2
    operators = jnp.concatenate([block_inverse, carry_gain], axis=0)
    near, far, diag = pack(adj_source, face_flux, face_owner, face_cell)
    messages = [
        exchange(diag, "blade", 3),
        exchange(near, "blade", 1),
        exchange(far, "blade", 2),
    ]
    chip = stack(operators, exchange(operators, "span", 1))
    apart = lax.ppermute(chip, "span", [(i, i ^ (2 + 2 * (i % 2))) for i in range(count)])
    farthest = exchange(operators, "span", 6)
    first, second = (4, 5, 6, 3), (2, 7, 1, 0)
    start = face_sums(first, circum, block_rows, far)
    start = face_sums(first, circum, block_rows, messages[2], start)
    *pieces, token = right_pieces(
        first, False, adj_source, start, messages, [], "right_first"
    )
    right_side = dict(zip(first, pieces, strict=True))
    across = stack(apart, farthest, token)
    partner = exchange(across, "span", 1)
    weights = call(
        operators_kernel,
        (((count, 2 * block_rows, 2 * block_rows), BF16),),
        [VMEM] * 3,
        [],
        0,
        "operators",
    )(chip, across, partner)[0]
    *pieces, _ = right_pieces(
        second, True, adj_source, far, messages, [token, weights], "right_second"
    )
    right_side |= dict(zip(second, pieces, strict=True))
    far_peers, near_peers = range(half, count), range(half)
    far_right = [exchange(right_side[i], "span", i) for i in far_peers]
    near_right = [right_side[0]] + [exchange(right_side[i], "span", i) for i in near_peers[1:]]

    rows = circum + 16
    right = pltpu.VMEM((half, rows, block_rows), F32)
    solved = pltpu.VMEM((half, circum, block_rows), F32)
    state_shape = ((ITERS, rows, block_rows), F32)
    piece = ((circum, block_rows), F32)
    state, done = call(
        functools.partial(lower_kernel, half, (6, 5, 3, 2)),
        (state_shape, ((half, circum, block_rows), F32)),
        [ANY, ANY, VMEM, VMEM, ANY, VMEM, VMEM, VMEM],
        [right],
        1_000_000_000,
        "sweeps_lower",
    )(far_right[0], far_right[1], near_right[3], near_right[2], far_right[2], near_right[1], near_right[0], weights)
    *far_solved, state = call(
        functools.partial(far_kernel, half),
        (piece,) * half + (state_shape,),
        [VMEM] * (half + 2),
        [right, solved],
        1_000_000_000,
        "sweeps_far",
    )(*far_right, weights, state)
    far_solved = [exchange(p, "span", i) for p, i in zip(far_solved, far_peers, strict=True)]
    near_solved = call(
        functools.partial(upper_kernel, half),
        (piece,) * half,
        [VMEM] * (half + 3),
        [right, solved],
        1_000_000_000,
        "sweeps_upper",
    )(*near_right, weights, state, done)
    near_solved = [p if i == 0 else exchange(p, "span", i) for i, p in enumerate(near_solved)]
    order = (4, 5, 6, 3, 2, 7, 1, 0)
    pieces = [*near_solved, *far_solved]
    return call(
        functools.partial(place_kernel, order),
        (((count, circum, block_rows), F32),),
        [ANY] * count,
        [pltpu.SemaphoreType.DMA((count,))],
        0,
        "place",
        out_specs=(ANY,),
    )(*[pieces[i] for i in order])[0]


def extended(block, sides, width):
    for axis, dim in sides:
        count = lax.axis_size(axis)
        forward = [(i, i + 1) for i in range(count - 1)]
        forward.append((count - 1, 0))
        backward = [(target, source) for source, target in forward]
        low = lax.ppermute(
            lax.slice_in_dim(block, block.shape[dim] - width, None, axis=dim), axis, forward
        )
        high = lax.ppermute(lax.slice_in_dim(block, 0, width, axis=dim), axis, backward)
        block = jnp.concatenate([low, block, high], axis=dim)
    return block


def pencil_solve(pencil, blocks, gains):
    harm_rows, columns, radial = pencil.shape
    nblocks, block_rows, _ = blocks.shape
    lines_all = pencil.reshape(harm_rows * columns, nblocks, block_rows)
    product = jnp.einsum("ckj,kij->kci", lines_all, blocks, precision=highest)

    def advance(running, element):
        local_part, gain = element
        updated = local_part + lax.dot_general(
            running,
            gain,
            (((1,), (1,)), ((), ())),
            precision=highest,
            preferred_element_type=jnp.float32,
        )
        return (updated, updated)

    initial = jnp.zeros((harm_rows * columns, block_rows), jnp.float32)
    _, solved = lax.scan(advance, initial, (product, gains))
    return jnp.transpose(solved, (1, 0, 2)).reshape(harm_rows, columns, radial)


def row_rhs(right_side, field):
    widened = extended(field, (("blade", 1),), 1)
    return right_side + coupling * (widened[:, :-2, :] + widened[:, 2:, :])


def by_lines(adj_source, face_flux, face_owner, face_cell, block_inverse, carry_gain):
    harm_rows, circum, block_rows = adj_source.shape
    blades = lax.axis_size("blade")
    faces_dev = face_owner.shape[0]
    capacity = faces_dev // 2
    onehot = (face_owner[:, None] == jnp.arange(blades, dtype=jnp.int32)[None, :]).astype(jnp.int32)
    rank_in = jnp.sum((jnp.cumsum(onehot, axis=0) - 1) * onehot, axis=1)
    slot_ids = face_owner * capacity + rank_in
    send_flux = (
        jnp.zeros((harm_rows, blades * capacity), jnp.float32)
        .at[:, slot_ids]
        .set(face_flux)
        .reshape(harm_rows, blades, capacity)
    )
    send_cell = (
        jnp.zeros((blades * capacity,), jnp.int32)
        .at[slot_ids]
        .set(face_cell)
        .reshape(1, blades, capacity)
    )
    fluxes, cell_ids = (
        lax.all_to_all(send_flux, "blade", split_axis=1, concat_axis=1, tiled=True),
        lax.all_to_all(send_cell, "blade", split_axis=1, concat_axis=1, tiled=True),
    )
    fluxes = fluxes.reshape(harm_rows, blades * capacity)
    cell_ids = cell_ids.reshape(blades * capacity)
    wall_flux = jnp.zeros((harm_rows, circum * block_rows), jnp.float32).at[:, cell_ids].add(fluxes)
    right_side = adj_source + wall_flux.reshape(harm_rows, circum, block_rows)
    inverses, couplings = (
        lax.all_gather(block_inverse, "span", axis=0, tiled=True),
        lax.all_gather(carry_gain, "span", axis=0, tiled=True),
    )
    blocks = inverses.reshape(-1, block_rows, block_rows)
    gains = couplings.reshape(-1, block_rows, block_rows)

    def transposed(rhs_rows):
        pencil = lax.all_to_all(rhs_rows, "span", split_axis=1, concat_axis=2, tiled=True)
        return lax.all_to_all(
            pencil_solve(pencil, blocks, gains), "span", split_axis=2, concat_axis=1, tiled=True
        )

    field = transposed(right_side)
    for sweep_index in range(1, ITERS):
        field = transposed(row_rhs(right_side, field))
    return field


def body(adj_source, *others):
    harm_rows, circum, block_rows = adj_source.shape
    if lax.axis_size("span") == harm_rows == 8 and lax.axis_size("blade") == 4:
        return by_harmonics(adj_source, *others)
    return by_lines(adj_source, *others)


def solution(mesh):
    in_specs = (
        P(None, "blade", "span"),
        P(None, ("blade", "span")),
        P(("blade", "span")),
        P(("blade", "span")),
        P("span", None),
        P("span", None),
    )
    out_specs = P(None, "blade", "span")
    return jax.shard_map(body, mesh=mesh, in_specs=in_specs, out_specs=out_specs, check_vma=False)
```
